256 devices in a mesh: dp: 8 (over y_lo, x), ctx: 32 (over y_hi, z, core).
Axes of the slice: x: 4, y: 4 (y_hi: 2, y_lo: 2; y = y_hi * 2 + y_lo), z: 8, core: 2. Of those that a mesh axis runs over, the one named last changes fastest.
Arguments:
- master: float32 [2048, 2560], P(('dp', 'ctx')), may hold values from -1 to 1
- moment1: float32 [2048, 2560], P(('dp', 'ctx')), may hold values from -0.3 to 0.3
- moment2: float32 [2048, 2560], P(('dp', 'ctx')), may hold values from 0.0001 to 0.01
- gradient: float32 [2048, 2560], P(('dp', 'ctx')), may hold values from -0.3 to 0.3
- tokens: bfloat16 [8, 8192, 2048], P('dp', 'ctx'), may hold values from -6 to 6
- gain: float32 [2048], replicated, may hold values from 0.5 to 1.5
- positions: int32 [8, 8192], P('dp', 'ctx'), may hold values from 0 to 8191, each once within a row
Outputs:
- new_master: float32 [2048, 2560], P(('dp', 'ctx'))
- new_moment1: float32 [2048, 2560], P(('dp', 'ctx'))
- new_moment2: float32 [2048, 2560], P(('dp', 'ctx'))
- block_out: bfloat16 [8, 8192, 2048], P('dp', 'ctx')
The draws below stay inside these ranges and needn't reach their ends.
Inputs may be any that keep to these rules, and one draw needn't show every extreme that they name: `positions`: each row is a permutation of 0 to 8191.
All inputs are finite; a program needn't handle non-finite values.
Results may differ from the reference program's by a relative error of at most 0.012.
The reference program's roundings to bfloat16 on the way count: a program that leaves them out, or rounds other values in their place, can miss the bound.
Values may be sent and summed in bfloat16 or wider, within the bound.
No kernel may reach another device: no remote copies, remote signals or barrier semaphores. Data moves between devices by JAX's collectives and lax.ppermute only.
A program may use at most 128 MiB of HBM per device.

```python
import math
import jax
import jax.numpy as jnp
from jax import lax

MODEL_WIDTH = 2048
HEAD_SIZE = 64
QUERY_HEADS = 16
KEY_VALUE_HEADS = 4
STEP = 100
SEQS = 8
SEQUENCE_TOKENS = 8192
COLS = 2560


def draw_master(key, part):
    key = jax.random.fold_in(key, 7)
    column_total = jnp.arange(COLS)
    fanout_width = jnp.where(column_total < (QUERY_HEADS + 2 * KEY_VALUE_HEADS) * HEAD_SIZE, float(MODEL_WIDTH), float(QUERY_HEADS * HEAD_SIZE))
    value_rows = jax.random.normal(key, (MODEL_WIDTH, COLS), jnp.float32)
    return value_rows / jnp.sqrt(fanout_width)


def block_scale(rng, shape, shards, least, high):
    level, own = 1.0, jax.random.fold_in(rng, 6)
    for axis_at, blocks in shards:
        heights = jnp.exp(jax.random.uniform(jax.random.fold_in(own, axis_at), (blocks,), jnp.float32, least / len(shards), high / len(shards)))
        level = level * jnp.repeat(heights, shape[axis_at] // blocks).reshape([-1 if axis == axis_at else 1 for axis in range(len(shape))])
    return level


def centred(rng, shape, width, reach, split=(), held_as=jnp.bfloat16):
    result = jax.random.normal(rng, shape, jnp.float32) * width
    if len(split) > 0:
        result = block_scale(rng, shape, split, -0.22, 0.18) * result
    return jnp.clip(result, min=-reach, max=reach).astype(held_as)


def setup_inputs(seed: int = 0) -> dict:
    keys = jax.random.split(jax.random.key(seed), 8)
    master = draw_master(jax.random.fold_in(keys[7], 71), 0)
    moment1 = centred(keys[1], (MODEL_WIDTH, COLS), 0.05, 0.3, ((0, 256),), jnp.float32)
    moment2 = jnp.clip(jnp.exp(math.log(0.01) - 4.6051702 * jax.random.uniform(keys[2], (MODEL_WIDTH, COLS), jnp.float32) ** block_scale(keys[2], (MODEL_WIDTH, COLS), ((0, 256),), -0.2, 0.2)), 0.0001, 0.01)
    gradient = centred(keys[3], (MODEL_WIDTH, COLS), 0.05, 0.3, ((0, 256),), jnp.float32)
    tokens = centred(keys[4], (SEQS, SEQUENCE_TOKENS, MODEL_WIDTH), 1.0, 6.0, ((0, 8), (1, 32)))
    gain = jnp.clip(1.0 + 0.1 * jax.random.normal(keys[5], (MODEL_WIDTH,), jnp.float32), 0.5, 1.5)
    positions = jax.vmap(lambda own: jax.random.permutation(own, SEQUENCE_TOKENS))(jax.random.split(keys[6], SEQS)).reshape((SEQS, SEQUENCE_TOKENS)).astype(jnp.int32)
    return dict(master=master, moment1=moment1, moment2=moment2, gradient=gradient, tokens=tokens, gain=gain, positions=positions)


beta_one = 0.9
beta_two = 0.95
learn_rate = 0.002
decay_rate = 0.1
epsilon = 1e-08

def head_attention(operands, order):
    query_head, key_head, value_head = operands
    scores = jnp.dot(query_head, key_head.T, preferred_element_type=jnp.float32) / jnp.sqrt(jnp.float32(HEAD_SIZE))
    visible = order[None, :] <= order[:, None]
    highest = lax.optimization_barrier(jnp.max(jnp.where(visible, scores, -jnp.inf), axis=1, keepdims=True))
    probs = jnp.where(visible, jnp.exp(scores - highest), 0.0)
    rowsum = lax.optimization_barrier(jnp.sum(probs, axis=1, keepdims=True))
    mixed = jnp.dot(probs.astype(jnp.bfloat16), value_head, preferred_element_type=jnp.float32)
    return mixed / rowsum

def sequence_attention(operands):
    packed_weights, order = operands
    query_span_width = QUERY_HEADS * HEAD_SIZE
    query_group = QUERY_HEADS // KEY_VALUE_HEADS
    query_rows = packed_weights[:, :query_span_width].reshape(SEQUENCE_TOKENS, QUERY_HEADS, HEAD_SIZE).transpose(1, 0, 2)
    key_rows = packed_weights[:, query_span_width:query_span_width + KEY_VALUE_HEADS * HEAD_SIZE].reshape(SEQUENCE_TOKENS, KEY_VALUE_HEADS, HEAD_SIZE).transpose(1, 0, 2)
    value_rows = packed_weights[:, query_span_width + KEY_VALUE_HEADS * HEAD_SIZE:].reshape(SEQUENCE_TOKENS, KEY_VALUE_HEADS, HEAD_SIZE).transpose(1, 0, 2)
    key_rows = jnp.repeat(key_rows, query_group, axis=0)
    value_rows = jnp.repeat(value_rows, query_group, axis=0)
    heads = lax.map(lambda item: head_attention(item, order), (query_rows, key_rows, value_rows))
    return heads.transpose(1, 0, 2).reshape(SEQUENCE_TOKENS, query_span_width).astype(jnp.bfloat16)

def reference(master, moment1, moment2, gradient, tokens, gain, positions):
    new_moment1 = beta_one * moment1 + (1.0 - beta_one) * gradient
    new_moment2 = beta_two * moment2 + (1.0 - beta_two) * gradient * gradient
    first_corr = 1.0 - beta_one ** STEP
    second_corr = 1.0 - beta_two ** STEP
    update = new_moment1 / first_corr / (jnp.sqrt(new_moment2 / second_corr) + epsilon)
    new_master = master - learn_rate * (update + decay_rate * master)
    weights = new_master.astype(jnp.bfloat16)
    query_key_value_width = (QUERY_HEADS + 2 * KEY_VALUE_HEADS) * HEAD_SIZE
    wide = tokens.astype(jnp.float32)
    meansq = lax.optimization_barrier(jnp.mean(wide * wide, axis=-1, keepdims=True))
    normed = (wide * lax.rsqrt(meansq + 1e-05) * gain).astype(jnp.bfloat16)
    query_key_value = jnp.dot(normed.reshape(SEQS * SEQUENCE_TOKENS, MODEL_WIDTH), weights[:, :query_key_value_width], preferred_element_type=jnp.float32)
    query_key_value = query_key_value.astype(jnp.bfloat16).reshape(SEQS, SEQUENCE_TOKENS, query_key_value_width)
    attention = lax.map(sequence_attention, (query_key_value, positions))
    block_out = lax.dot_general(attention.reshape(SEQS * SEQUENCE_TOKENS, QUERY_HEADS * HEAD_SIZE), weights[:, query_key_value_width:], (((1,), (1,)), ((), ())), preferred_element_type=jnp.float32)
    block_out = block_out.astype(jnp.bfloat16).reshape(SEQS, SEQUENCE_TOKENS, MODEL_WIDTH)
    return (new_master, new_moment1, new_moment2, block_out)
```

```python
import functools
import math

import jax
import jax.numpy as jnp
from jax import lax
from jax.experimental import pallas as pl
from jax.experimental.pallas import tpu as pltpu
from jax.sharding import PartitionSpec as P

STEP = 100
beta_one = 0.9
beta_two = 0.95
learn_rate = 0.002
decay_rate = 0.1
epsilon = 1e-08

AXES = ("dp", "ctx")
BF = jnp.bfloat16
F32 = jnp.float32
MIB = 1 << 20
HALF = 528
TILES = 16
KEYS = 256
LOG2E = math.log2(math.e)


def device_of(x, y, z, core):
    x, y, z = x % 4, y % 4, z % 8
    return ((y % 2) * 4 + x) * 32 + (y // 2) * 16 + z * 2 + core


def moved(target):
    return [
        (device_of(x, y, z, c), device_of(*target(x, y, z, c)))
        for x in range(4)
        for y in range(4)
        for z in range(8)
        for c in range(2)
    ]


CORE = moved(lambda x, y, z, c: (x, y, z, 1 - c))
Y_HI = moved(lambda x, y, z, c: (x, y + 2, z, c))
DIAG = moved(lambda x, y, z, c: (x, y + 2, z, 1 - c))
Y_LO = moved(lambda x, y, z, c: (x, y ^ 1, z, c))
X_UP = moved(lambda x, y, z, c: (x + 1, y, z, c))
X_DOWN = moved(lambda x, y, z, c: (x - 1, y, z, c))
X_FAR = moved(lambda x, y, z, c: (x + 2, y, z, c))
Z_UP = moved(lambda x, y, z, c: (x, y, z + 1, c))
Z_DOWN = moved(lambda x, y, z, c: (x, y, z - 1, c))


def send(value, perm):
    return lax.ppermute(value, AXES, perm)


VMEM = pl.BlockSpec(memory_space=pltpu.VMEM)
SMEM = pl.BlockSpec(memory_space=pltpu.SMEM)


def call(kernel, out, args, specs, limit=32, flops=0, scratch=(), aliases=None):
    moved_bytes = sum(a.size * a.dtype.itemsize for a in args)
    return pl.pallas_call(
        kernel,
        out_shape=out,
        in_specs=specs,
        out_specs=jax.tree.map(lambda _: VMEM, out),
        scratch_shapes=list(scratch),
        input_output_aliases=aliases or {},
        cost_estimate=pl.CostEstimate(
            flops=flops, bytes_accessed=moved_bytes, transcendentals=0
        ),
        compiler_params=pltpu.CompilerParams(vmem_limit_bytes=limit * MIB),
    )(*args)


def lanes(shape):
    return lax.broadcasted_iota(jnp.int32, shape, len(shape) - 1)


def rows(shape):
    return lax.broadcasted_iota(jnp.int32, shape, len(shape) - 2)


def dot(a, b):
    return jnp.dot(a, b, preferred_element_type=F32)


def first_kernel(
    master, moment1, moment2, gradient, tokens, gain, pos, nm, n1, n2, sent, normed
):
    g = gradient[...]
    m1 = beta_one * moment1[...] + (1.0 - beta_one) * g
    m2 = beta_two * moment2[...] + (1.0 - beta_two) * g * g
    update = m1 / (1.0 - beta_one**STEP) / (jnp.sqrt(m2 / (1.0 - beta_two**STEP)) + epsilon)
    old = master[...]
    new = old - learn_rate * (update + decay_rate * old)
    nm[...] = new
    n1[...] = m1
    n2[...] = m2
    low = lanes((8, 128)) < 64
    line = rows((8, 128))
    digits = jnp.zeros((8, 128), F32)
    for u in range(2):
        p = pos[:, u * 128 : (u + 1) * 128]
        hi = lax.shift_right_logical(p, 6).astype(F32)
        lo = lax.bitwise_and(p, 63).astype(F32)
        digits = jnp.where(line == u, hi, jnp.where(line == 2 + u, lo, digits))
    for y_hi in range(2):
        pair = []
        for c in range(2):
            h = y_hi * 2 + c
            kt = new[:, 1024 + y_hi * 128 : 1152 + y_hi * 128]
            vt = new[:, 1280 + y_hi * 128 : 1408 + y_hi * 128]
            if c == 0:
                kv = jnp.where(low, kt, pltpu.roll(vt, 64, 1))
            else:
                kv = jnp.where(low, pltpu.roll(kt, 64, 1), vt)
            pair.append(
                jnp.concatenate(
                    [
                        new[:, h * 256 : (h + 1) * 256],
                        kv,
                        new[:, 1536 + h * 256 : 1792 + h * 256],
                        digits,
                    ],
                    axis=1,
                )
            )
        both = jnp.concatenate(pair, axis=0).astype(BF)
        for z in range(8):
            at = y_hi * 128 + z * 16
            sent[at : at + 16, :] = both
    scale = gain[...]
    for r in range(0, 256, 64):
        wide = tokens[r : r + 64, :].astype(F32)
        meansq = jnp.mean(wide * wide, axis=1, keepdims=True)
        normed[r : r + 64, :] = (wide * lax.rsqrt(meansq + 1e-05) * scale).astype(BF)


def order_kernel(place, posd, perm, perm_t, posq, posk, counts, wide):
    ctx = place[1]
    wide[...] = posd[...].astype(F32)

    def pieces(j):
        eight = wide[pl.ds(pl.multiple_of(j * 8, 8), 8), :]
        return [eight[u : u + 1, :] * 64.0 + eight[2 + u : 3 + u, :] for u in range(2)]

    row = []
    for other in (0, 1, 16, 17):
        row += pieces(lax.bitwise_xor(ctx, other))
    col = [jnp.broadcast_to(r, (128, 128)).T for r in row]
    at_row = rows((128, 128)).astype(F32)
    at_lane = lanes((128, 128)).astype(F32)
    rank_row = []
    for b in range(8):
        below = jnp.zeros((128, 128), F32)
        for a in range(8):
            below = below + jnp.where(col[a] < row[b], 1.0, 0.0)
        rank_row.append(jnp.sum(below, axis=0, keepdims=True))
    rank_col = [jnp.broadcast_to(r, (128, 128)).T for r in rank_row]
    for a in range(8):
        total = jnp.zeros((128, 128), F32)
        for b in range(8):
            hit = at_row + float(a * 128) == rank_row[b]
            perm[a * 128 : (a + 1) * 128, b * 128 : (b + 1) * 128] = jnp.where(
                hit, 1.0, 0.0
            ).astype(BF)
            total = total + jnp.where(hit, row[b], 0.0)
        posq[a * 128 : (a + 1) * 128, :] = jnp.broadcast_to(
            jnp.sum(total, axis=1, keepdims=True), (128, 128)
        )
    for c in range(8):
        total = jnp.zeros((128, 128), F32)
        for a in range(8):
            hit = at_lane + float(c * 128) == rank_col[a]
            perm_t[a * 128 : (a + 1) * 128, c * 128 : (c + 1) * 128] = jnp.where(
                hit, 1.0, 0.0
            ).astype(BF)
            total = total + jnp.where(hit, col[a], 0.0)
        posk[c : c + 1, :] = jnp.sum(total, axis=0, keepdims=True)
    most = jnp.concatenate([posq[64 * t + 63 : 64 * t + 64, :] for t in range(TILES)], axis=0)
    least = jnp.concatenate([posq[64 * t : 64 * t + 1, :] for t in range(TILES)], axis=0)
    result = jnp.zeros((TILES, 128), F32)
    lane = lanes((TILES, 128))
    for z in range(8):
        some = jnp.zeros((TILES, 128), F32)
        full = jnp.zeros((TILES, 128), F32)
        for other in (0, 1, 16, 17):
            for piece in pieces(z * 2 + other):
                some = some + jnp.where(piece <= most, 1.0, 0.0)
                full = full + jnp.where(piece <= least, 1.0, 0.0)
        some = jnp.sum(some, axis=1, keepdims=True)
        full = jnp.sum(full, axis=1, keepdims=True)
        result = jnp.where(lane == z, some, jnp.where(lane == 8 + z, full, result))
    counts[...] = result.astype(jnp.int32)


def project(place, tokens, weights, s):
    dp = place[0]
    y_lo, x = lax.div(dp, 4), lax.rem(dp, 4)
    total = None
    for block, step in zip(weights, (0, 3, 1, 2)):
        other = lax.rem(x + step, 4)
        for r in range(2):
            owner = (y_lo if r == 0 else 1 - y_lo) * 4 + other
            part = tokens[s][:, pl.ds(pl.multiple_of(owner * 256, 256), 256)]
            term = dot(part, block[r * 256 : (r + 1) * 256, :])
            total = term if total is None else total + term
    return total.astype(BF)


def key_kernel(place, perm, posk, t0, t1, t2, t3, w0, w1, w2, w3, out, held):
    for s in range(4):
        held[s * 256 : (s + 1) * 256, :] = project(place, (t0, t1, t2, t3), (w0, w1, w2, w3), s)
    for r in range(4):
        ordered = dot(perm[r * 256 : (r + 1) * 256, :], held[...]).astype(BF)
        at = (r // 2) * HALF + (r % 2) * 256
        out[at : at + 256, :] = ordered
    p = posk[...]
    high = jnp.floor(p * (1.0 / 64.0))
    low = p - high * 64.0
    none = jnp.zeros((4, 128), F32)
    for u in range(2):
        digits = jnp.concatenate(
            [high[u * 4 : u * 4 + 4], none, low[u * 4 : u * 4 + 4], none], axis=0
        )
        out[u * HALF + 512 : (u + 1) * HALF, :] = digits.astype(BF)


def query_kernel(place, perm, t0, t1, t2, t3, w0, w1, w2, w3, out, held):
    for s in range(4):
        held[s * 256 : (s + 1) * 256, :] = project(place, (t0, t1, t2, t3), (w0, w1, w2, w3), s)
    low = lanes((64, 128)) < 64
    for r in range(4):
        ordered = dot(perm[r * 256 : (r + 1) * 256, :], held[...]) * (LOG2E / 8.0)
        for i in range(4):
            tile = r * 4 + i
            for j in range(2):
                q = ordered[i * 64 : (i + 1) * 64, j * 128 : (j + 1) * 128]
                hi = q.astype(BF).astype(F32)
                lo = q - hi
                first = jnp.where(low, hi, pltpu.roll(lo, 64, 1)).astype(BF)
                second = jnp.where(low, pltpu.roll(hi, 64, 1), lo).astype(BF)
                at = tile * 256 + j * 128
                out[at : at + 64, :] = first
                out[at + 64 : at + 128, :] = second


def attend_kernel(halves, first, last, *refs):
    refs = list(refs)
    place, counts, q, posq = refs[:4]
    del refs[:4]
    n_refs = 1 + max(h[0] for h in halves)
    blocks = refs[:n_refs]
    del refs[:n_refs]
    if not first:
        m_in, acc_in = refs[:2]
        del refs[:2]
    if last:
        perm_t = refs.pop(0)
        outs = refs[:4]
        del refs[:4]
        held, acc_ref = refs[3:]
    else:
        m_ref, acc_ref = refs[:2]
        del refs[:2]
    kk, v1, pk = refs[:3]
    low = lanes((512, 128)) < 64
    for i, (n, at, _, _) in enumerate(halves):
        kv = blocks[n][at : at + 512, :].astype(F32)
        kk[i * 512 : (i + 1) * 512, :] = jnp.where(low, kv, pltpu.roll(kv, 64, 1)).astype(BF)
        v1[i * 512 : (i + 1) * 512, :] = jnp.where(low, 1.0, kv).astype(BF)
        digits = blocks[n][at + 512 : at + 528, :].astype(F32)
        p = digits[0:4] * 64.0 + digits[8:12]
        for j in range(2):
            line = jnp.concatenate([p[2 * j : 2 * j + 1], p[2 * j + 1 : 2 * j + 2]], axis=1)
            k = i * 2 + j
            pk[k * 8 : (k + 1) * 8, :] = jnp.broadcast_to(line, (8, KEYS))
    z = lax.rem(lax.div(place[1], 2), 8)

    def tile_step(t, _):
        base = pl.multiple_of(t * 256, 256)
        qt = q[pl.ds(base, 256), :]
        pq = posq[pl.ds(pl.multiple_of(t * 64, 64), 64), :]
        pq = jnp.concatenate([pq] * 4, axis=0)
        pq = jnp.concatenate([pq, pq], axis=1)
        if first:
            m = jnp.full((256, 128), -1e29, F32)
            acc = jnp.zeros((256, 128), F32)
        else:
            m = (m_in)[pl.ds(base, 256), :]
            acc = (acc_in)[pl.ds(base, 256), :]

        def step(masked, k, state):
            m, acc = state
            at = pl.multiple_of(k * KEYS, KEYS)
            s = lax.dot_general(
                qt, kk[pl.ds(at, KEYS), :], (((1,), (1,)), ((), ())), preferred_element_type=F32
            )
            if masked:
                line = pk[pl.ds(pl.multiple_of(k * 8, 8), 8), :][0:1]
                s = jnp.where(line <= pq, s, -1e30)
            high = jnp.maximum(m, jnp.max(s, axis=1, keepdims=True))
            p = jnp.exp2(s - jnp.concatenate([high, high], axis=1))
            acc = acc * jnp.exp2(m - high) + dot(p.astype(BF), v1[pl.ds(at, KEYS), :])
            return high, acc

        state = (m, acc)
        for i, (_, _, away, u) in enumerate(halves):
            other = lax.rem(z + away + 8, 8)
            some = jnp.clip(counts[t, other] - u * 512, 0, 512)
            full = jnp.clip(counts[t, 8 + other] - u * 512, 0, 512)
            n_some = lax.div(some + (KEYS - 1), KEYS)
            n_full = lax.div(full, KEYS)
            state = lax.fori_loop(
                i * 2, i * 2 + n_full, functools.partial(step, False), state
            )
            state = lax.fori_loop(
                i * 2 + n_full, i * 2 + n_some, functools.partial(step, True), state
            )
        m, acc = state
        if not last:
            m_ref[pl.ds(base, 256), :] = m
        acc_ref[pl.ds(base, 256), :] = acc
        return 0

    lax.fori_loop(0, TILES, tile_step, 0)
    if last:
        low = lanes((64, 128)) < 64
        for t in range(TILES):
            for j in range(2):
                at = t * 256 + j * 128
                a = acc_ref[at : at + 64, :]
                b = acc_ref[at + 64 : at + 128, :]
                up = pltpu.roll(a, 64, 1) / a
                down = b / pltpu.roll(b, 64, 1)
                held[t * 64 : (t + 1) * 64, j * 128 : (j + 1) * 128] = jnp.where(
                    low, up, down
                ).astype(BF)
        for s in range(4):
            outs[s][...] = dot(perm_t[s * 256 : (s + 1) * 256, :], held[...]).astype(BF)


def out_kernel(place, a0, a1, a2, a3, w0, w1, w2, w3, out):
    dp = place[0]
    y_lo, x = lax.div(dp, 4), lax.rem(dp, 4)
    for n, step in enumerate((0, 3, 1, 2)):
        other = lax.rem(x + step, 4)
        for r in range(2):
            owner = (y_lo if r == 0 else 1 - y_lo) * 4 + other
            at = n * 512 + r * 256
            total = None
            for a, w in ((a0, w0), (a1, w1), (a2, w2), (a3, w3)):
                term = lax.dot_general(
                    a[...], w[at : at + 256, :], (((1,), (1,)), ((), ())), preferred_element_type=F32
                )
                total = term if total is None else total + term
            out[:, pl.ds(pl.multiple_of(owner * 256, 256), 256)] = total.astype(BF)


def spread(block):
    pair = jnp.concatenate([block, send(block, Y_LO)], axis=0)
    return pair, send(pair, X_UP), send(pair, X_DOWN), send(pair, X_FAR)


def attend(place, counts, q, posq, blocks, halves, state, perm_t=None):
    first, last = state is None, perm_t is not None
    args = [place, counts, q, posq, *blocks]
    specs = [SMEM, SMEM] + [VMEM] * (2 + len(blocks))
    aliases = {}
    if not first:
        if not last:
            aliases = {len(args): 0, len(args) + 1: 1}
        args += state
        specs += [VMEM] * 2
    n = len(halves)
    scratch = [
        pltpu.VMEM((n * 512, 128), BF),
        pltpu.VMEM((n * 512, 128), BF),
        pltpu.VMEM((n * 16, KEYS), F32),
    ]
    if last:
        args.append(perm_t)
        specs.append(VMEM)
        out = [jax.ShapeDtypeStruct((256, 256), BF)] * 4
        scratch += [pltpu.VMEM((1024, 256), BF), pltpu.VMEM((4096, 128), F32)]
    else:
        out = [jax.ShapeDtypeStruct((4096, 128), F32)] * 2
    return call(
        functools.partial(attend_kernel, halves, first, last),
        out,
        args,
        specs,
        flops=n * 4096 * 512 * 64 * 8,
        scratch=scratch,
        aliases=aliases,
    )


def body(master, moment1, moment2, gradient, tokens, gain, positions):
    place = jnp.stack([lax.axis_index("dp"), lax.axis_index("ctx")]).astype(jnp.int32)
    shard = jax.ShapeDtypeStruct(master.shape, F32)
    new_master, new_moment1, new_moment2, sent, normed = call(
        first_kernel,
        [
            shard,
            shard,
            shard,
            jax.ShapeDtypeStruct((256, 768), BF),
            jax.ShapeDtypeStruct((256, 2048), BF),
        ],
        [
            master,
            moment1,
            moment2,
            gradient,
            tokens.reshape(256, 2048),
            gain.reshape(1, 2048),
            positions,
        ],
        [VMEM] * 7,
    )
    by_y = send(normed, Y_HI)
    by_core = send(normed, CORE)
    by_both = send(by_y, CORE)
    slots = [normed, by_core, by_y, by_both]
    mine = lax.all_to_all(sent, "ctx", 0, 0, tiled=True)
    weights_kv = spread(mine[:, 256:384])
    weights_q = spread(mine[:, :256])
    posd = mine[:, 640:768]
    perm, perm_t, posq, posk, counts = call(
        order_kernel,
        [
            jax.ShapeDtypeStruct((1024, 1024), BF),
            jax.ShapeDtypeStruct((1024, 1024), BF),
            jax.ShapeDtypeStruct((1024, 128), F32),
            jax.ShapeDtypeStruct((8, 128), F32),
            jax.ShapeDtypeStruct((TILES, 128), jnp.int32),
        ],
        [place, posd],
        [SMEM, VMEM],
        scratch=[pltpu.VMEM((256, 128), F32)],
    )
    block = call(
        key_kernel,
        jax.ShapeDtypeStruct((2 * HALF, 128), BF),
        [place, perm, posk, *slots, *weights_kv],
        [SMEM] + [VMEM] * 10,
        flops=2 * 1024 * 3072 * 128,
        scratch=[pltpu.VMEM((1024, 128), BF)],
    )
    q = call(
        query_kernel,
        jax.ShapeDtypeStruct((4096, 128), BF),
        [place, perm, *slots, *weights_q],
        [SMEM] + [VMEM] * 9,
        flops=2 * 1024 * 3072 * 256,
        scratch=[pltpu.VMEM((1024, 256), BF)],
    )
    own = [(0, 0, 0, 0), (0, HALF, 0, 1)]
    state = attend(place, counts, q, posq, [block], own, None)
    up, down = block, block
    for step in range(1, 4):
        up, down = send(up, Z_UP), send(down, Z_DOWN)
        halves = [
            (0, 0, -step, 0),
            (0, HALF, -step, 1),
            (1, 0, step, 0),
            (1, HALF, step, 1),
        ]
        state = attend(place, counts, q, posq, [up, down], halves, state)
    far = [send(up[:HALF], Z_UP), send(down[HALF:], Z_DOWN)]
    parts = attend(
        place, counts, q, posq, far, [(0, 0, 4, 0), (1, 0, 4, 1)], state, perm_t
    )
    out_own = jnp.concatenate(spread(mine[:, 384:640]), axis=0)
    out_y = send(out_own, Y_HI)
    out_core = send(out_own, CORE)
    out_both = send(out_y, CORE)
    heads = [parts[0], send(parts[1], CORE), send(parts[2], Y_HI), send(parts[3], DIAG)]
    block_out = call(
        out_kernel,
        jax.ShapeDtypeStruct((256, 2048), BF),
        [place, *heads, out_own, out_core, out_y, out_both],
        [SMEM] + [VMEM] * 8,
        flops=2 * 256 * 1024 * 2048,
    )
    return new_master, new_moment1, new_moment2, block_out.reshape(1, 256, 2048)


def solution(mesh):
    rows_split = P(AXES, None)
    return jax.shard_map(
        body,
        mesh=mesh,
        in_specs=(
            rows_split,
            rows_split,
            rows_split,
            rows_split,
            P("dp", "ctx", None),
            P(),
            P("dp", "ctx"),
        ),
        out_specs=(rows_split, rows_split, rows_split, P("dp", "ctx", None)),
        check_vma=False,
    )
```

```python
import functools

import jax
import jax.numpy as jnp
from jax import lax
from jax.experimental import pallas as pl
from jax.experimental.pallas import tpu as pltpu
from jax.sharding import PartitionSpec as P

STEP = 100
beta_one = 0.9
beta_two = 0.95
learn_rate = 0.002
decay_rate = 0.1
epsilon = 1e-08

AXES = ("dp", "ctx")
BF = jnp.bfloat16
F32 = jnp.float32
MIB = 1 << 20
HALF = 528
TILES = 4
WIDE = 1024
KEYS = 256


def device_of(x, y, z, core):
    x, y, z = x % 4, y % 4, z % 8
    return ((y % 2) * 4 + x) * 32 + (y // 2) * 16 + z * 2 + core


def moved(target):
    return [
        (device_of(x, y, z, c), device_of(*target(x, y, z, c)))
        for x in range(4)
        for y in range(4)
        for z in range(8)
        for c in range(2)
    ]


CORE = moved(lambda x, y, z, c: (x, y, z, 1 - c))
Y_HI = moved(lambda x, y, z, c: (x, y + 2, z, c))
DIAG = moved(lambda x, y, z, c: (x, y + 2, z, 1 - c))
Y_LO = moved(lambda x, y, z, c: (x, y ^ 1, z, c))
X_UP = moved(lambda x, y, z, c: (x + 1, y, z, c))
X_DOWN = moved(lambda x, y, z, c: (x - 1, y, z, c))
X_FAR = moved(lambda x, y, z, c: (x + 2, y, z, c))
Z_UP = moved(lambda x, y, z, c: (x, y, z + 1, c))
Z_DOWN = moved(lambda x, y, z, c: (x, y, z - 1, c))


def send(value, perm):
    return lax.ppermute(value, AXES, perm)


VMEM = pl.BlockSpec(memory_space=pltpu.VMEM)
SMEM = pl.BlockSpec(memory_space=pltpu.SMEM)
HBM = pl.BlockSpec(memory_space=pltpu.HBM)


def call(kernel, out, args, specs, limit=32, flops=0, scratch=(), aliases=None):
    moved_bytes = sum(a.size * a.dtype.itemsize for a in args)
    return pl.pallas_call(
        kernel,
        out_shape=out,
        in_specs=specs,
        out_specs=jax.tree.map(lambda _: VMEM, out),
        scratch_shapes=list(scratch),
        input_output_aliases=aliases or {},
        cost_estimate=pl.CostEstimate(
            flops=flops, bytes_accessed=moved_bytes, transcendentals=0
        ),
        compiler_params=pltpu.CompilerParams(vmem_limit_bytes=limit * MIB),
    )(*args)


def lanes(shape):
    return lax.broadcasted_iota(jnp.int32, shape, len(shape) - 1)


def rows(shape):
    return lax.broadcasted_iota(jnp.int32, shape, len(shape) - 2)


def dot(a, b):
    return jnp.dot(a, b, preferred_element_type=F32)


def norm_kernel(tokens, gain, normed):
    scale = gain[...]
    for r in range(0, 256, 64):
        wide = tokens[r : r + 64, :].astype(F32)
        meansq = jnp.mean(wide * wide, axis=1, keepdims=True)
        normed[r : r + 64, :] = (wide * lax.rsqrt(meansq + 1e-05) * scale).astype(BF)


def adam_kernel(
    master_hbm, moment1_hbm, moment2_hbm, gradient_hbm, pos_hbm, after, nm, n1, n2, sent, held, pos, sems
):
    del after
    copies = [
        pltpu.make_async_copy(ref, held.at[i], sems.at[i])
        for i, ref in enumerate((master_hbm, moment1_hbm, moment2_hbm, gradient_hbm))
    ]
    copies.append(pltpu.make_async_copy(pos_hbm, pos, sems.at[4]))
    for copy in copies:
        copy.start()
    for copy in copies:
        copy.wait()
    g = held[3]
    m1 = beta_one * held[1] + (1.0 - beta_one) * g
    m2 = beta_two * held[2] + (1.0 - beta_two) * g * g
    update = m1 / (1.0 - beta_one**STEP) / (jnp.sqrt(m2 / (1.0 - beta_two**STEP)) + epsilon)
    old = held[0]
    new = old - learn_rate * (update + decay_rate * old)
    nm[...] = new
    n1[...] = m1
    n2[...] = m2
    low = lanes((8, 128)) < 64
    line = rows((8, 128))
    digits = jnp.zeros((8, 128), F32)
    for u in range(2):
        p = pos[:, u * 128 : (u + 1) * 128]
        hi = lax.shift_right_logical(p, 6).astype(F32)
        lo = lax.bitwise_and(p, 63).astype(F32)
        digits = jnp.where(line == u, hi, jnp.where(line == 2 + u, lo, digits))
    for y_hi in range(2):
        pair = []
        for c in range(2):
            h = y_hi * 2 + c
            kt = new[:, 1024 + y_hi * 128 : 1152 + y_hi * 128]
            vt = new[:, 1280 + y_hi * 128 : 1408 + y_hi * 128]
            if c == 0:
                kv = jnp.where(low, kt, pltpu.roll(vt, 64, 1))
            else:
                kv = jnp.where(low, pltpu.roll(kt, 64, 1), vt)
            pair.append(
                jnp.concatenate(
                    [
                        new[:, h * 256 : (h + 1) * 256],
                        kv,
                        new[:, 1536 + h * 256 : 1792 + h * 256],
                        digits,
                    ],
                    axis=1,
                )
            )
        both = jnp.concatenate(pair, axis=0).astype(BF)
        for z in range(8):
            at = y_hi * 128 + z * 16
            sent[at : at + 16, :] = both


def order_kernel(place, posd, perm, perm_t, posq, posk, counts, wide):
    ctx = place[1]
    wide[...] = posd[...].astype(F32)

    def pieces(j):
        eight = wide[pl.ds(pl.multiple_of(j * 8, 8), 8), :]
        return [eight[u : u + 1, :] * 64.0 + eight[2 + u : 3 + u, :] for u in range(2)]

    row = []
    for other in (0, 1, 16, 17):
        row += pieces(lax.bitwise_xor(ctx, other))
    col = [jnp.broadcast_to(r, (128, 128)).T for r in row]
    at_row = rows((128, 128)).astype(F32)
    at_lane = lanes((128, 128)).astype(F32)
    rank_row = []
    for b in range(8):
        below = jnp.zeros((128, 128), F32)
        for a in range(8):
            below = below + jnp.where(col[a] < row[b], 1.0, 0.0)
        rank_row.append(jnp.sum(below, axis=0, keepdims=True))
    rank_col = [jnp.broadcast_to(r, (128, 128)).T for r in rank_row]
    for a in range(8):
        for b in range(8):
            hit = at_row + float(a * 128) == rank_row[b]
            perm[a * 128 : (a + 1) * 128, b * 128 : (b + 1) * 128] = jnp.where(
                hit, 1.0, 0.0
            ).astype(BF)
    ordered = []
    for c in range(8):
        total = jnp.zeros((128, 128), F32)
        for a in range(8):
            hit = at_lane + float(c * 128) == rank_col[a]
            perm_t[a * 128 : (a + 1) * 128, c * 128 : (c + 1) * 128] = jnp.where(
                hit, 1.0, 0.0
            ).astype(BF)
            total = total + jnp.where(hit, col[a], 0.0)
        ordered.append(jnp.sum(total, axis=0, keepdims=True))
        posk[c : c + 1, :] = ordered[c]
    line = rows((8, 128))
    lane = lanes((8, 128))
    most = jnp.zeros((8, 128), F32)
    for t in range(TILES):
        tile = jnp.concatenate(ordered[2 * t : 2 * t + 2] * 4, axis=1)
        posq[t * 8 : (t + 1) * 8, :] = jnp.broadcast_to(tile, (8, WIDE))
        top = jnp.max(ordered[2 * t + 1], axis=1, keepdims=True)
        most = jnp.where(line == t, jnp.broadcast_to(top, (8, 128)), most)
    result = jnp.zeros((8, 128), F32)
    for z in range(8):
        some = jnp.zeros((8, 128), F32)
        for other in (0, 1, 16, 17):
            for piece in pieces(z * 2 + other):
                some = some + jnp.where(piece <= most, 1.0, 0.0)
        result = jnp.where(lane == z, jnp.sum(some, axis=1, keepdims=True), result)
    counts[...] = result.astype(jnp.int32)


def project(place, tokens, weights, s):
    dp = place[0]
    y_lo, x = lax.div(dp, 4), lax.rem(dp, 4)
    total = None
    for block, step in zip(weights, (0, 3, 1, 2)):
        other = lax.rem(x + step, 4)
        for r in range(2):
            owner = (y_lo if r == 0 else 1 - y_lo) * 4 + other
            part = tokens[s][:, pl.ds(pl.multiple_of(owner * 256, 256), 256)]
            term = dot(part, block[r * 256 : (r + 1) * 256, :])
            total = term if total is None else total + term
    return total.astype(BF)


def key_kernel(place, perm, posk, t0, t1, t2, t3, w0, w1, w2, w3, out, held):
    for s in range(4):
        held[s * 256 : (s + 1) * 256, :] = project(place, (t0, t1, t2, t3), (w0, w1, w2, w3), s)
    low = lanes((256, 128)) < 64
    p = posk[...]
    high = jnp.floor(p * (1.0 / 64.0))
    rest = p - high * 64.0
    none = jnp.zeros((4, 128), F32)
    for u in range(2):
        at = u * HALF
        a, b = [dot(perm[r * 256 : (r + 1) * 256, :], held[...]) for r in (2 * u, 2 * u + 1)]
        out[at : at + 256, :] = jnp.where(low, a, pltpu.roll(b, 64, 1)).astype(BF)
        for c in range(4):
            piece = (a if c < 2 else b)[(c % 2) * 128 : (c % 2) * 128 + 128]
            out[at + 256 + c * 64 : at + 320 + c * 64, :] = piece.T[64:].astype(BF)
        digits = jnp.concatenate(
            [high[u * 4 : u * 4 + 4], none, rest[u * 4 : u * 4 + 4], none], axis=0
        )
        out[at + 512 : at + HALF, :] = digits.astype(BF)


def query_kernel(place, perm, t0, t1, t2, t3, w0, w1, w2, w3, out, held):
    for s in range(4):
        held[s * 256 : (s + 1) * 256, :] = project(place, (t0, t1, t2, t3), (w0, w1, w2, w3), s)
    for t in range(TILES):
        ordered = dot(perm[t * 256 : (t + 1) * 256, :], held[...]) * 0.125
        for i in range(2):
            for j in range(2):
                q = ordered[i * 128 : (i + 1) * 128, j * 128 : (j + 1) * 128].T
                for e in range(2):
                    lane = (j * 2 + e) * 256 + i * 128
                    out[t * 64 : (t + 1) * 64, lane : lane + 128] = q[
                        e * 64 : (e + 1) * 64
                    ].astype(BF)


def attend_kernel(blocks, first, last, *refs):
    refs = list(refs)
    place, counts, q, posq = refs[:4]
    del refs[:4]
    n_refs = 1 + max(n for _, halves in blocks for n, _ in halves)
    held = refs[:n_refs]
    del refs[:n_refs]
    if not first:
        m_in, acc_in = refs[:2]
        del refs[:2]
    if last:
        perm_t = refs.pop(0)
        outs = refs[:4]
        del refs[:4]
        kk, v1, pk, scores, mixed = refs
    else:
        m_ref, acc_ref, kk, v1, pk, scores = refs
    lines = []
    n = 0
    for _, halves in blocks:
        for ref, at in halves:
            a = held[ref][at : at + 256, :].astype(F32)
            b = pltpu.roll(a, 64, 1)
            kk[n * 512 : n * 512 + 256, :] = a.astype(BF)
            kk[n * 512 + 256 : n * 512 + 512, :] = b.astype(BF)
            for c in range(4):
                v1[0:64, n * 512 + c * 128 : n * 512 + (c + 1) * 128] = held[ref][
                    at + 256 + c * 64 : at + 320 + c * 64, :
                ]
            digits = held[ref][at + 512 : at + HALF, :].astype(F32)
            lines.append(digits[0:8] * 64.0 + digits[8:16])
            n += 1
    v1[64:80, :] = jnp.ones((16, n * 512), BF)
    lines.append(jnp.zeros((128 - 8 * n, 128), F32))
    columns = jnp.concatenate(lines, axis=0).T
    for i in range(n):
        for c in range(4):
            k = i * 4 + c
            pk[k * 128 : (k + 1) * 128, :] = jnp.broadcast_to(
                columns[:, i * 8 + c : i * 8 + c + 1], (128, 128)
            )
    z = lax.rem(lax.div(place[1], 2), 8)

    def tile_step(t, _):
        qt = q[pl.ds(pl.multiple_of(t * 64, 64), 64), :]
        pq = posq[pl.ds(pl.multiple_of(t * 8, 8), 8), :][0:1]
        m_at = pl.ds(pl.multiple_of(t * 8, 8), 8)
        acc_at = pl.ds(pl.multiple_of(t * 80, 16), 80)
        if first:
            m = jnp.full((1, WIDE), -1e29, F32)
            acc = jnp.zeros((80, WIDE), F32)
        else:
            m = m_in[m_at, :][0:1]
            acc = acc_in[acc_at, :]

        def some(base, steps, state):
            m, acc = state
            high = m
            for j in range(steps):
                at = base + j * KEYS
                s = dot(kk[at : at + KEYS, 0:64], qt)
                line = jnp.concatenate([pk[at : at + KEYS, :]] * (WIDE // 128), axis=1)
                s = jnp.where(line <= pq, s, -1e30)
                scores[j] = s
                high = jnp.maximum(high, jnp.max(s, axis=0, keepdims=True))
            acc = acc * jnp.exp(m - high)
            for j in range(steps):
                at = base + j * KEYS
                p = jnp.exp(scores[j] - high).astype(BF)
                acc = acc + dot(v1[:, at : at + KEYS], p)
            return high, acc

        state = (m, acc)
        for i, (away, _) in enumerate(blocks):
            other = lax.rem(z + away + 8, 8)
            steps = lax.div(counts[t, other] + (KEYS - 1), KEYS)
            branches = [functools.partial(some, i * 1024, k) for k in range(1024 // KEYS + 1)]
            branches[0] = lambda state: state
            state = lax.switch(steps, branches, state)
        m, acc = state
        if last:
            o = acc[0:64] / acc[64:65]
            for h in range(4):
                mixed[h * 64 : (h + 1) * 64, pl.ds(pl.multiple_of(t * 256, 256), 256)] = o[
                    :, h * 256 : (h + 1) * 256
                ].astype(BF)
        else:
            m_ref[m_at, :] = jnp.broadcast_to(m, (8, WIDE))
            acc_ref[acc_at, :] = acc
        return 0

    lax.fori_loop(0, TILES, tile_step, 0)
    if last:
        for s in range(4):
            outs[s][...] = lax.dot_general(
                perm_t[s * 256 : (s + 1) * 256, :],
                mixed[...],
                (((1,), (1,)), ((), ())),
                preferred_element_type=F32,
            ).astype(BF)


def out_kernel(a0, a1, a2, a3, w_own, w_core, out):
    for owner in range(8):
        total = None
        for a, w, r in ((a0, w_own, 0), (a1, w_core, 0), (a2, w_own, 1), (a3, w_core, 1)):
            at = owner * 512 + r * 256
            term = lax.dot_general(
                a[...], w[at : at + 256, :], (((1,), (1,)), ((), ())), preferred_element_type=F32
            )
            total = term if total is None else total + term
        out[:, owner * 256 : (owner + 1) * 256] = total.astype(BF)


def after(value, other):
    return lax.optimization_barrier((value, other))[0]


def spread(block, near, before):
    pair = jnp.concatenate([block, near], axis=0)
    return pair, send(pair, X_UP), send(pair, X_DOWN), send(after(pair, before), X_FAR)


def attend(place, counts, q, posq, held, blocks, state, perm_t=None):
    first, last = state is None, perm_t is not None
    args = [place, counts, q, posq, *held]
    specs = [SMEM, SMEM] + [VMEM] * (2 + len(held))
    aliases = {}
    if not first:
        if not last:
            aliases = {len(args): 0, len(args) + 1: 1}
        args += state
        specs += [VMEM] * 2
    n = len(blocks)
    scratch = [
        pltpu.VMEM((n * 1024, 128), BF),
        pltpu.VMEM((80, n * 1024), BF),
        pltpu.VMEM((n * 1024, 128), F32),
        pltpu.VMEM((1024 // KEYS, KEYS, WIDE), F32),
    ]
    if last:
        args.append(perm_t)
        specs.append(VMEM)
        out = [jax.ShapeDtypeStruct((256, 256), BF)] * 4
        scratch.append(pltpu.VMEM((256, 1024), BF))
    else:
        out = [
            jax.ShapeDtypeStruct((TILES * 8, WIDE), F32),
            jax.ShapeDtypeStruct((TILES * 80, WIDE), F32),
        ]
    return call(
        functools.partial(attend_kernel, blocks, first, last),
        out,
        args,
        specs,
        flops=n * 4096 * 1024 * 64 * 8,
        scratch=scratch,
        aliases=aliases,
    )


def body(master, moment1, moment2, gradient, tokens, gain, positions):
    place = jnp.stack([lax.axis_index("dp"), lax.axis_index("ctx")]).astype(jnp.int32)
    shard = jax.ShapeDtypeStruct(master.shape, F32)
    normed = call(
        norm_kernel,
        jax.ShapeDtypeStruct((256, 2048), BF),
        [tokens.reshape(256, 2048), gain.reshape(1, 2048)],
        [VMEM] * 2,
    )
    by_y = send(normed, Y_HI)
    by_core = send(normed, CORE)
    new_master, new_moment1, new_moment2, sent = call(
        adam_kernel,
        [shard, shard, shard, jax.ShapeDtypeStruct((256, 768), BF)],
        [master, moment1, moment2, gradient, positions, normed],
        [HBM] * 5 + [pl.BlockSpec(memory_space=pl.ANY)],
        scratch=[
            pltpu.VMEM((4, 8, 2560), F32),
            pltpu.VMEM((1, 256), jnp.int32),
            pltpu.SemaphoreType.DMA((5,)),
        ],
    )
    mine = lax.all_to_all(sent, "ctx", 0, 0, tiled=True)
    posd = mine[:, 640:768]
    perm, perm_t, posq, posk, counts = call(
        order_kernel,
        [
            jax.ShapeDtypeStruct((1024, 1024), BF),
            jax.ShapeDtypeStruct((1024, 1024), BF),
            jax.ShapeDtypeStruct((TILES * 8, WIDE), F32),
            jax.ShapeDtypeStruct((8, 128), F32),
            jax.ShapeDtypeStruct((8, 128), jnp.int32),
        ],
        [place, posd],
        [SMEM, VMEM],
        scratch=[pltpu.VMEM((256, 128), F32)],
    )
    mine_kv = mine[:, 256:384]
    near_kv = send(mine_kv, Y_LO)
    slots = [normed, by_core, by_y, send(by_y, CORE)]
    near_q = send(mine[:, :256], Y_LO)
    weights_kv = spread(mine_kv, after(near_kv, counts), near_q)
    weights_q = spread(mine[:, :256], after(near_q, weights_kv[1]), near_q)
    mine_out = after(mine[:, 384:640], near_q)
    out_pair = jnp.concatenate([mine_out, send(mine_out, Y_HI)], axis=0)
    block = call(
        key_kernel,
        jax.ShapeDtypeStruct((2 * HALF, 128), BF),
        [place, perm, posk, *slots, *weights_kv],
        [SMEM] + [VMEM] * 10,
        flops=2 * 1024 * 3072 * 128,
        scratch=[pltpu.VMEM((1024, 128), BF)],
    )
    q = call(
        query_kernel,
        jax.ShapeDtypeStruct((TILES * 64, WIDE), BF),
        [place, perm, *slots, *weights_q],
        [SMEM] + [VMEM] * 9,
        flops=2 * 1024 * 3072 * 256,
        scratch=[pltpu.VMEM((1024, 256), BF)],
    )
    def whole(ref):
        return ((ref, 0), (ref, HALF))

    state = attend(place, counts, q, posq, [block], [(0, whole(0))], None)
    up, down = block, block
    for step in range(1, 4):
        up, down = send(up, Z_UP), send(down, Z_DOWN)
        if step == 1:
            out_own = lax.all_gather(after(out_pair, (up, down, q)), "dp", axis=0, tiled=True)
        state = attend(
            place, counts, q, posq, [up, down], [(-step, whole(0)), (step, whole(1))], state
        )
    far = [send(up[:HALF], Z_UP), send(down[HALF:], Z_DOWN)]
    parts = attend(
        place, counts, q, posq, far, [(4, ((0, 0), (1, 0)))], state, perm_t
    )
    out_core = send(after(out_own, parts[0]), CORE)
    heads = [parts[0], send(parts[1], CORE), send(parts[2], Y_HI), send(parts[3], DIAG)]
    block_out = call(
        out_kernel,
        jax.ShapeDtypeStruct((256, 2048), BF),
        [*heads, out_own, out_core],
        [VMEM] * 6,
        flops=2 * 256 * 1024 * 2048,
    )
    return new_master, new_moment1, new_moment2, block_out.reshape(1, 256, 2048)


def solution(mesh):
    rows_split = P(AXES, None)
    return jax.shard_map(
        body,
        mesh=mesh,
        in_specs=(
            rows_split,
            rows_split,
            rows_split,
            rows_split,
            P("dp", "ctx", None),
            P(),
            P("dp", "ctx"),
        ),
        out_specs=(rows_split, rows_split, rows_split, P("dp", "ctx", None)),
        check_vma=False,
    )
```

```python
import functools

import jax
import jax.numpy as jnp
from jax import lax
from jax.experimental import pallas as pl
from jax.experimental.pallas import tpu as pltpu
from jax.sharding import PartitionSpec as P

STEP = 100
beta_one = 0.9
beta_two = 0.95
learn_rate = 0.002
decay_rate = 0.1
epsilon = 1e-08

AXES = ("dp", "ctx")
BF = jnp.bfloat16
F32 = jnp.float32
MIB = 1 << 20
HALF = 528
TILES = 4
WIDE = 1024
KEYS = 256


def device_of(x, y, z, core):
    x, y, z = x % 4, y % 4, z % 8
    return ((y % 2) * 4 + x) * 32 + (y // 2) * 16 + z * 2 + core


def moved(target):
    return [
        (device_of(x, y, z, c), device_of(*target(x, y, z, c)))
        for x in range(4)
        for y in range(4)
        for z in range(8)
        for c in range(2)
    ]


CORE = moved(lambda x, y, z, c: (x, y, z, 1 - c))
Y_HI = moved(lambda x, y, z, c: (x, y + 2, z, c))
DIAG = moved(lambda x, y, z, c: (x, y + 2, z, 1 - c))
Y_LO = moved(lambda x, y, z, c: (x, y ^ 1, z, c))
X_UP = moved(lambda x, y, z, c: (x + 1, y, z, c))
X_DOWN = moved(lambda x, y, z, c: (x - 1, y, z, c))
X_FAR = moved(lambda x, y, z, c: (x + 2, y, z, c))
Z_UP = moved(lambda x, y, z, c: (x, y, z + 1, c))
Z_DOWN = moved(lambda x, y, z, c: (x, y, z - 1, c))


def send(value, perm):
    return lax.ppermute(value, AXES, perm)


VMEM = pl.BlockSpec(memory_space=pltpu.VMEM)
SMEM = pl.BlockSpec(memory_space=pltpu.SMEM)
HBM = pl.BlockSpec(memory_space=pltpu.HBM)


def call(kernel, out, args, specs, limit=32, flops=0, scratch=(), aliases=None):
    moved_bytes = sum(a.size * a.dtype.itemsize for a in args)
    return pl.pallas_call(
        kernel,
        out_shape=out,
        in_specs=specs,
        out_specs=jax.tree.map(lambda _: VMEM, out),
        scratch_shapes=list(scratch),
        input_output_aliases=aliases or {},
        cost_estimate=pl.CostEstimate(
            flops=flops, bytes_accessed=moved_bytes, transcendentals=0
        ),
        compiler_params=pltpu.CompilerParams(vmem_limit_bytes=limit * MIB),
    )(*args)


def lanes(shape):
    return lax.broadcasted_iota(jnp.int32, shape, len(shape) - 1)


def rows(shape):
    return lax.broadcasted_iota(jnp.int32, shape, len(shape) - 2)


def dot(a, b):
    return jnp.dot(a, b, preferred_element_type=F32)


def norm_kernel(tokens, gain, normed):
    scale = gain[...]
    for r in range(0, 256, 64):
        wide = tokens[r : r + 64, :].astype(F32)
        meansq = jnp.mean(wide * wide, axis=1, keepdims=True)
        normed[r : r + 64, :] = (wide * lax.rsqrt(meansq + 1e-05) * scale).astype(BF)


def adam_kernel(
    master_hbm, moment1_hbm, moment2_hbm, gradient_hbm, pos_hbm, after, nm, n1, n2, sent, held, pos, sems
):
    del after
    copies = [
        pltpu.make_async_copy(ref, held.at[i], sems.at[i])
        for i, ref in enumerate((master_hbm, moment1_hbm, moment2_hbm, gradient_hbm))
    ]
    copies.append(pltpu.make_async_copy(pos_hbm, pos, sems.at[4]))
    for copy in copies:
        copy.start()
    for copy in copies:
        copy.wait()
    g = held[3]
    m1 = beta_one * held[1] + (1.0 - beta_one) * g
    m2 = beta_two * held[2] + (1.0 - beta_two) * g * g
    update = m1 / (1.0 - beta_one**STEP) / (jnp.sqrt(m2 / (1.0 - beta_two**STEP)) + epsilon)
    old = held[0]
    new = old - learn_rate * (update + decay_rate * old)
    nm[...] = new
    n1[...] = m1
    n2[...] = m2
    low = lanes((8, 128)) < 64
    line = rows((8, 128))
    digits = jnp.zeros((8, 128), F32)
    for u in range(2):
        p = pos[:, u * 128 : (u + 1) * 128]
        hi = lax.shift_right_logical(p, 6).astype(F32)
        lo = lax.bitwise_and(p, 63).astype(F32)
        digits = jnp.where(line == u, hi, jnp.where(line == 2 + u, lo, digits))
    for y_hi in range(2):
        pair = []
        for c in range(2):
            h = y_hi * 2 + c
            kt = new[:, 1024 + y_hi * 128 : 1152 + y_hi * 128]
            vt = new[:, 1280 + y_hi * 128 : 1408 + y_hi * 128]
            if c == 0:
                kv = jnp.where(low, kt, pltpu.roll(vt, 64, 1))
            else:
                kv = jnp.where(low, pltpu.roll(kt, 64, 1), vt)
            pair.append(
                jnp.concatenate(
                    [
                        new[:, h * 256 : (h + 1) * 256],
                        kv,
                        new[:, 1536 + h * 256 : 1792 + h * 256],
                        digits,
                    ],
                    axis=1,
                )
            )
        both = jnp.concatenate(pair, axis=0).astype(BF)
        for z in range(8):
            at = y_hi * 128 + z * 16
            sent[at : at + 16, :] = both


def order_kernel(place, posd, perm, posq, posk, counts, wide):
    ctx = place[1]
    wide[...] = posd[...].astype(F32)

    def pieces(j):
        eight = wide[pl.ds(pl.multiple_of(j * 8, 8), 8), :]
        return [(eight[u : u + 1, :], eight[2 + u : 3 + u, :]) for u in range(2)]

    digits = []
    for other in (0, 1, 16, 17):
        digits += pieces(lax.bitwise_xor(ctx, other))
    row = [hi * 64.0 + lo for hi, lo in digits]
    col = [jnp.broadcast_to(r, (128, 128)).T for r in row]
    at_row = rows((128, 128)).astype(F32)
    for b in range(8):
        below = jnp.zeros((128, 128), F32)
        for a in range(8):
            below = below + jnp.where(col[a] < row[b], 1.0, 0.0)
        rank = jnp.sum(below, axis=0, keepdims=True)
        for a in range(8):
            perm[a * 128 : (a + 1) * 128, b * 128 : (b + 1) * 128] = jnp.where(
                at_row + float(a * 128) == rank, 1.0, 0.0
            ).astype(BF)
    line = rows((16, 1024))
    high = jnp.concatenate([hi for hi, _ in digits], axis=1)
    low = jnp.concatenate([lo for _, lo in digits], axis=1)
    both = jnp.where(line == 0, high, jnp.where(line == 1, low, 0.0)).astype(BF)
    both = lax.dot_general(
        both, perm[...], (((1,), (1,)), ((), ())), preferred_element_type=F32
    )
    ordered = both[0:1] * 64.0 + both[1:2]
    line = rows((8, 128))
    lane = lanes((8, 128))
    most = jnp.zeros((8, 128), F32)
    for c in range(8):
        posk[c : c + 1, :] = ordered[:, c * 128 : (c + 1) * 128]
    for t in range(TILES):
        tile = ordered[:, t * 256 : (t + 1) * 256]
        posq[t * 8 : (t + 1) * 8, :] = jnp.broadcast_to(
            jnp.concatenate([tile] * 4, axis=1), (8, WIDE)
        )
        top = jnp.max(tile[:, 128:], axis=1, keepdims=True)
        most = jnp.where(line == t, jnp.broadcast_to(top, (8, 128)), most)
    result = jnp.zeros((8, 128), F32)
    for z in range(8):
        some = jnp.zeros((8, 128), F32)
        for other in (0, 1, 16, 17):
            for hi, lo in pieces(z * 2 + other):
                some = some + jnp.where(hi * 64.0 + lo <= most, 1.0, 0.0)
        result = jnp.where(lane == z, jnp.sum(some, axis=1, keepdims=True), result)
    counts[...] = result.astype(jnp.int32)


def project(place, tokens, weights, s):
    dp = place[0]
    y_lo, x = lax.div(dp, 4), lax.rem(dp, 4)
    total = None
    for block, step in zip(weights, (0, 3, 1, 2)):
        other = lax.rem(x + step, 4)
        for r in range(2):
            owner = (y_lo if r == 0 else 1 - y_lo) * 4 + other
            part = tokens[s][:, pl.ds(pl.multiple_of(owner * 256, 256), 256)]
            term = dot(part, block[r * 256 : (r + 1) * 256, :])
            total = term if total is None else total + term
    return total.astype(BF)


def project_kernel(place, perm, posk, t0, t1, t2, t3, w0, w1, w2, w3, out, queries, held):
    for s in range(4):
        held[s * 256 : (s + 1) * 256, :] = project(place, (t0, t1, t2, t3), (w0, w1, w2, w3), s)
    low = lanes((256, 128)) < 64
    p = posk[...]
    high = jnp.floor(p * (1.0 / 64.0))
    rest = p - high * 64.0
    none = jnp.zeros((4, 128), F32)
    kept = None
    for t in range(TILES):
        u = t // 2
        at = u * HALF
        ordered = dot(perm[t * 256 : (t + 1) * 256, :], held[...])
        kv = ordered[:, 256:]
        if t % 2 == 0:
            kept = kv
        else:
            out[at : at + 256, :] = jnp.where(low, kept, pltpu.roll(kv, 64, 1)).astype(BF)
        for i in range(2):
            c = (t % 2) * 2 + i
            out[at + 256 + c * 64 : at + 320 + c * 64, :] = kv[
                i * 128 : (i + 1) * 128
            ].T[64:].astype(BF)
            for j in range(2):
                q = ordered[i * 128 : (i + 1) * 128, j * 128 : (j + 1) * 128].T * 0.125
                for e in range(2):
                    lane = (j * 2 + e) * 256 + i * 128
                    queries[t * 64 : (t + 1) * 64, lane : lane + 128] = q[
                        e * 64 : (e + 1) * 64
                    ].astype(BF)
    for u in range(2):
        digits = jnp.concatenate(
            [high[u * 4 : u * 4 + 4], none, rest[u * 4 : u * 4 + 4], none], axis=0
        )
        out[u * HALF + 512 : (u + 1) * HALF, :] = digits.astype(BF)


def attend_kernel(blocks, first, last, *refs):
    refs = list(refs)
    place, counts, q, posq = refs[:4]
    del refs[:4]
    n_refs = 1 + max(n for _, halves in blocks for n, _ in halves)
    held = refs[:n_refs]
    del refs[:n_refs]
    if not first:
        m_in, acc_in = refs[:2]
        del refs[:2]
    if last:
        perm = refs.pop(0)
        outs = refs[:4]
        del refs[:4]
        kk, v1, pk, scores, mixed = refs
    else:
        m_ref, acc_ref, kk, v1, pk, scores = refs
    lines = []
    n = 0
    for _, halves in blocks:
        for ref, at in halves:
            a = held[ref][at : at + 256, :].astype(F32)
            b = pltpu.roll(a, 64, 1)
            kk[n * 512 : n * 512 + 256, :] = a.astype(BF)
            kk[n * 512 + 256 : n * 512 + 512, :] = b.astype(BF)
            for c in range(4):
                v1[0:64, n * 512 + c * 128 : n * 512 + (c + 1) * 128] = held[ref][
                    at + 256 + c * 64 : at + 320 + c * 64, :
                ]
            digits = held[ref][at + 512 : at + HALF, :].astype(F32)
            lines.append(digits[0:8] * 64.0 + digits[8:16])
            n += 1
    v1[64:80, :] = jnp.ones((16, n * 512), BF)
    lines.append(jnp.zeros((128 - 8 * n, 128), F32))
    columns = jnp.concatenate(lines, axis=0).T
    for i in range(n):
        for c in range(4):
            k = i * 4 + c
            pk[k * 128 : (k + 1) * 128, :] = jnp.broadcast_to(
                columns[:, i * 8 + c : i * 8 + c + 1], (128, 128)
            )
    z = lax.rem(lax.div(place[1], 2), 8)

    def tile_step(t, _):
        qt = q[pl.ds(pl.multiple_of(t * 64, 64), 64), :]
        pq = posq[pl.ds(pl.multiple_of(t * 8, 8), 8), :][0:1]
        m_at = pl.ds(pl.multiple_of(t * 8, 8), 8)
        acc_at = pl.ds(pl.multiple_of(t * 80, 16), 80)
        if first:
            m = jnp.full((1, WIDE), -1e29, F32)
            acc = jnp.zeros((80, WIDE), F32)
        else:
            m = m_in[m_at, :][0:1]
            acc = acc_in[acc_at, :]

        def some(base, steps, state):
            m, acc = state
            high = m
            for j in range(steps):
                at = base + j * KEYS
                s = dot(kk[at : at + KEYS, 0:64], qt)
                line = jnp.concatenate([pk[at : at + KEYS, :]] * (WIDE // 128), axis=1)
                s = jnp.where(line <= pq, s, -1e30)
                scores[j] = s
                high = jnp.maximum(high, jnp.max(s, axis=0, keepdims=True))
            acc = acc * jnp.exp(m - high)
            for j in range(steps):
                at = base + j * KEYS
                p = jnp.exp(scores[j] - high).astype(BF)
                acc = acc + dot(v1[:, at : at + KEYS], p)
            return high, acc

        state = (m, acc)
        for i, (away, _) in enumerate(blocks):
            other = lax.rem(z + away + 8, 8)
            steps = lax.div(counts[t, other] + (KEYS - 1), KEYS)
            branches = [functools.partial(some, i * 1024, k) for k in range(1024 // KEYS + 1)]
            branches[0] = lambda state: state
            state = lax.switch(steps, branches, state)
        m, acc = state
        if last:
            o = acc[0:64] / acc[64:65]
            for h in range(4):
                mixed[h * 64 : (h + 1) * 64, pl.ds(pl.multiple_of(t * 256, 256), 256)] = o[
                    :, h * 256 : (h + 1) * 256
                ].astype(BF)
        else:
            m_ref[m_at, :] = jnp.broadcast_to(m, (8, WIDE))
            acc_ref[acc_at, :] = acc
        return 0

    lax.fori_loop(0, TILES, tile_step, 0)
    if last:
        for s in range(4):
            back = dot(mixed[...], perm[:, s * 256 : (s + 1) * 256])
            outs[s][...] = back.T.astype(BF)


def out_kernel(place, a0, a1, a2, a3, w_own, w_core, out):
    dp = place[0]
    y_lo, x = lax.div(dp, 4), lax.rem(dp, 4)
    for n, step in enumerate((0, 3, 1, 2)):
        other = lax.rem(x + step, 4)
        for r in range(2):
            owner = (y_lo if r == 0 else 1 - y_lo) * 4 + other
            total = None
            for a, w, half in ((a0, w_own, 0), (a1, w_core, 0), (a2, w_own, 1), (a3, w_core, 1)):
                at = n * 1024 + r * 512 + half * 256
                term = lax.dot_general(
                    a[...], w[at : at + 256, :], (((1,), (1,)), ((), ())), preferred_element_type=F32
                )
                total = term if total is None else total + term
            out[:, pl.ds(pl.multiple_of(owner * 256, 256), 256)] = total.astype(BF)


def after(value, other):
    return lax.optimization_barrier((value, other))[0]


def spread(pair):
    return pair, send(pair, X_UP), send(pair, X_DOWN), send(pair, X_FAR)


def attend(place, counts, q, posq, held, blocks, state, perm=None):
    first, last = state is None, perm is not None
    args = [place, counts, q, posq, *held]
    specs = [SMEM, SMEM] + [VMEM] * (2 + len(held))
    aliases = {}
    if not first:
        if not last:
            aliases = {len(args): 0, len(args) + 1: 1}
        args += state
        specs += [VMEM] * 2
    n = len(blocks)
    scratch = [
        pltpu.VMEM((n * 1024, 128), BF),
        pltpu.VMEM((80, n * 1024), BF),
        pltpu.VMEM((n * 1024, 128), F32),
        pltpu.VMEM((1024 // KEYS, KEYS, WIDE), F32),
    ]
    if last:
        args.append(perm)
        specs.append(VMEM)
        out = [jax.ShapeDtypeStruct((256, 256), BF)] * 4
        scratch.append(pltpu.VMEM((256, 1024), BF))
    else:
        out = [
            jax.ShapeDtypeStruct((TILES * 8, WIDE), F32),
            jax.ShapeDtypeStruct((TILES * 80, WIDE), F32),
        ]
    return call(
        functools.partial(attend_kernel, blocks, first, last),
        out,
        args,
        specs,
        flops=n * 4096 * 1024 * 64 * 8,
        scratch=scratch,
        aliases=aliases,
    )


def body(master, moment1, moment2, gradient, tokens, gain, positions):
    place = jnp.stack([lax.axis_index("dp"), lax.axis_index("ctx")]).astype(jnp.int32)
    shard = jax.ShapeDtypeStruct(master.shape, F32)
    normed = call(
        norm_kernel,
        jax.ShapeDtypeStruct((256, 2048), BF),
        [tokens.reshape(256, 2048), gain.reshape(1, 2048)],
        [VMEM] * 2,
    )
    by_y = send(normed, Y_HI)
    by_core = send(normed, CORE)
    new_master, new_moment1, new_moment2, sent = call(
        adam_kernel,
        [shard, shard, shard, jax.ShapeDtypeStruct((256, 768), BF)],
        [master, moment1, moment2, gradient, positions, normed],
        [HBM] * 5 + [pl.BlockSpec(memory_space=pl.ANY)],
        scratch=[
            pltpu.VMEM((4, 8, 2560), F32),
            pltpu.VMEM((1, 256), jnp.int32),
            pltpu.SemaphoreType.DMA((5,)),
        ],
    )
    mine = lax.all_to_all(sent, "ctx", 0, 0, tiled=True)
    posd = mine[:, 640:768]
    perm, posq, posk, counts = call(
        order_kernel,
        [
            jax.ShapeDtypeStruct((1024, 1024), BF),
            jax.ShapeDtypeStruct((TILES * 8, WIDE), F32),
            jax.ShapeDtypeStruct((8, 128), F32),
            jax.ShapeDtypeStruct((8, 128), jnp.int32),
        ],
        [place, posd],
        [SMEM, VMEM],
        scratch=[pltpu.VMEM((256, 128), F32)],
    )
    mine_qkv = mine[:, :384]
    near = send(mine_qkv, Y_LO)
    slots = [normed, by_core, by_y, send(by_y, CORE)]
    pair = jnp.concatenate([mine_qkv, after(near, counts)], axis=0)
    weights = spread(pair)
    block, q = call(
        project_kernel,
        [
            jax.ShapeDtypeStruct((2 * HALF, 128), BF),
            jax.ShapeDtypeStruct((TILES * 64, WIDE), BF),
        ],
        [place, perm, posk, *slots, *weights],
        [SMEM] + [VMEM] * 10,
        flops=2 * 1024 * 3072 * 384,
        scratch=[pltpu.VMEM((1024, 384), BF)],
    )
    mine_out = after(mine[:, 384:640], weights[1])
    out_pair = jnp.concatenate([mine_out, send(mine_out, Y_HI)], axis=0)
    out_pair = jnp.concatenate([out_pair, send(out_pair, Y_LO)], axis=0)

    def whole(ref):
        return ((ref, 0), (ref, HALF))

    state = attend(place, counts, q, posq, [block], [(0, whole(0))], None)
    up, down = block, block
    for step in range(1, 4):
        up, down = send(up, Z_UP), send(down, Z_DOWN)
        if step == 1:
            out_own = jnp.concatenate(spread(after(out_pair, (up, down, state[0]))), axis=0)
        state = attend(
            place, counts, q, posq, [up, down], [(-step, whole(0)), (step, whole(1))], state
        )
    far = [send(up[:HALF], Z_UP), send(down[HALF:], Z_DOWN)]
    out_core = send(after(out_own, (far, state[0])), CORE)
    parts = attend(place, counts, q, posq, far, [(4, ((0, 0), (1, 0)))], state, perm)
    heads = [parts[0], send(parts[1], CORE), send(parts[2], Y_HI), send(parts[3], DIAG)]
    block_out = call(
        out_kernel,
        jax.ShapeDtypeStruct((256, 2048), BF),
        [place, *heads, out_own, out_core],
        [SMEM] + [VMEM] * 6,
        flops=2 * 256 * 1024 * 2048,
    )
    return new_master, new_moment1, new_moment2, block_out.reshape(1, 256, 2048)


def solution(mesh):
    rows_split = P(AXES, None)
    return jax.shard_map(
        body,
        mesh=mesh,
        in_specs=(
            rows_split,
            rows_split,
            rows_split,
            rows_split,
            P("dp", "ctx", None),
            P(),
            P("dp", "ctx"),
        ),
        out_specs=(rows_split, rows_split, rows_split, P("dp", "ctx", None)),
        check_vma=False,
    )
```

```python
import functools

import jax
import jax.numpy as jnp
from jax import lax
from jax.experimental import pallas as pl
from jax.experimental.pallas import tpu as pltpu
from jax.sharding import PartitionSpec as P

STEP = 100
beta_one = 0.9
beta_two = 0.95
learn_rate = 0.002
decay_rate = 0.1
epsilon = 1e-08

AXES = ("dp", "ctx")
BF = jnp.bfloat16
F32 = jnp.float32
MIB = 1 << 20
HALF = 528
TILES = 4
WIDE = 1024
KEYS = 256


def device_of(x, y, z, core):
    x, y, z = x % 4, y % 4, z % 8
    return ((y % 2) * 4 + x) * 32 + (y // 2) * 16 + z * 2 + core


def moved(target):
    return [
        (device_of(x, y, z, c), device_of(*target(x, y, z, c)))
        for x in range(4)
        for y in range(4)
        for z in range(8)
        for c in range(2)
    ]


CORE = moved(lambda x, y, z, c: (x, y, z, 1 - c))
Y_HI = moved(lambda x, y, z, c: (x, y + 2, z, c))
DIAG = moved(lambda x, y, z, c: (x, y + 2, z, 1 - c))
Y_LO = moved(lambda x, y, z, c: (x, y ^ 1, z, c))
X_UP = moved(lambda x, y, z, c: (x + 1, y, z, c))
X_DOWN = moved(lambda x, y, z, c: (x - 1, y, z, c))
X_FAR = moved(lambda x, y, z, c: (x + 2, y, z, c))
Z_UP = moved(lambda x, y, z, c: (x, y, z + 1, c))
Z_DOWN = moved(lambda x, y, z, c: (x, y, z - 1, c))


def send(value, perm):
    return lax.ppermute(value, AXES, perm)


VMEM = pl.BlockSpec(memory_space=pltpu.VMEM)
SMEM = pl.BlockSpec(memory_space=pltpu.SMEM)
HBM = pl.BlockSpec(memory_space=pltpu.HBM)


def call(kernel, out, args, specs, limit=32, flops=0, scratch=(), aliases=None):
    moved_bytes = sum(a.size * a.dtype.itemsize for a in args)
    return pl.pallas_call(
        kernel,
        out_shape=out,
        in_specs=specs,
        out_specs=jax.tree.map(lambda _: VMEM, out),
        scratch_shapes=list(scratch),
        input_output_aliases=aliases or {},
        cost_estimate=pl.CostEstimate(
            flops=flops, bytes_accessed=moved_bytes, transcendentals=0
        ),
        compiler_params=pltpu.CompilerParams(vmem_limit_bytes=limit * MIB),
    )(*args)


def lanes(shape):
    return lax.broadcasted_iota(jnp.int32, shape, len(shape) - 1)


def rows(shape):
    return lax.broadcasted_iota(jnp.int32, shape, len(shape) - 2)


def dot(a, b):
    return jnp.dot(a, b, preferred_element_type=F32)


def norm_kernel(tokens, gain, sent, normed):
    del sent
    scale = gain[...]
    for r in range(0, 256, 64):
        wide = tokens[r : r + 64, :].astype(F32)
        meansq = jnp.mean(wide * wide, axis=1, keepdims=True)
        normed[r : r + 64, :] = (wide * lax.rsqrt(meansq + 1e-05) * scale).astype(BF)


def adam_kernel(
    place,
    master_hbm,
    moment1_hbm,
    moment2_hbm,
    gradient_hbm,
    pos_hbm,
    nm,
    n1,
    n2,
    s0,
    s1,
    s2,
    s3,
    held,
    pos,
    sems,
):
    copies = [
        pltpu.make_async_copy(ref, held.at[i], sems.at[i])
        for i, ref in enumerate((master_hbm, moment1_hbm, moment2_hbm, gradient_hbm))
    ]
    copies.append(pltpu.make_async_copy(pos_hbm, pos, sems.at[4]))
    for copy in copies:
        copy.start()
    for copy in copies:
        copy.wait()
    g = held[3]
    m1 = beta_one * held[1] + (1.0 - beta_one) * g
    m2 = beta_two * held[2] + (1.0 - beta_two) * g * g
    update = m1 / (1.0 - beta_one**STEP) / (jnp.sqrt(m2 / (1.0 - beta_two**STEP)) + epsilon)
    old = held[0]
    new = old - learn_rate * (update + decay_rate * old)
    nm[...] = new
    n1[...] = m1
    n2[...] = m2
    low = lanes((8, 128)) < 64
    line = rows((8, 128))
    digits = jnp.zeros((8, 128), F32)
    for u in range(2):
        p = pos[:, u * 128 : (u + 1) * 128]
        hi = lax.shift_right_logical(p, 6).astype(F32)
        lo = lax.bitwise_and(p, 63).astype(F32)
        digits = jnp.where(line == u, hi, jnp.where(line == 2 + u, lo, digits))
    rounded = new.astype(BF).astype(F32)
    parts = []
    for h in range(4):
        at = (h // 2) * 128
        kt = rounded[:, 1024 + at : 1152 + at]
        vt = rounded[:, 1280 + at : 1408 + at]
        if h % 2 == 0:
            kv = jnp.where(low, kt, pltpu.roll(vt, 64, 1))
        else:
            kv = jnp.where(low, pltpu.roll(kt, 64, 1), vt)
        parts.append(
            jnp.concatenate(
                [
                    rounded[:, h * 256 : (h + 1) * 256],
                    kv,
                    rounded[:, 1536 + h * 256 : 1792 + h * 256],
                    digits,
                ],
                axis=1,
            )
        )
    ctx = place[1]
    mine = lax.div(ctx, 16) * 2 + lax.rem(ctx, 2)
    for s, ref in enumerate((s0, s1, s2, s3)):
        h = lax.bitwise_xor(mine, s)
        lower = jnp.where(h == 0, parts[0], parts[1])
        upper = jnp.where(h == 2, parts[2], parts[3])
        ref[...] = jnp.where(h < 2, lower, upper)


def repeat_kernel(r0, r1, r2, r3, normed, out):
    del normed
    block = jnp.concatenate([r0[...], r1[...], r2[...], r3[...]], axis=0).astype(BF)
    for z in range(8):
        out[z * 32 : (z + 1) * 32, :] = block


def place_kernel(place, mixed, qkv, out, posd):
    ctx = place[1]
    y_hi, core = lax.div(ctx, 16), lax.rem(ctx, 2)
    i = rows((256, 256))
    j = lax.shift_right_logical(i, 3)
    slot = lax.bitwise_xor(lax.shift_right_logical(j, 4), y_hi) * 2 + lax.bitwise_xor(
        lax.bitwise_and(j, 1), core
    )
    z = lax.bitwise_and(lax.shift_right_logical(j, 1), 7)
    source = z * 32 + slot * 8 + lax.bitwise_and(i, 7)
    pick = jnp.where(lanes((256, 256)) == source, 1.0, 0.0).astype(BF)
    result = dot(pick, mixed[...])
    qkv[...] = result[:, :384].astype(BF)
    out[...] = result[:, 384:640].astype(BF)
    posd[...] = result[:, 640:]


def order_kernel(place, posd, perm, posq, posk, counts):
    ctx = place[1]

    def pieces(j):
        eight = posd[pl.ds(pl.multiple_of(j * 8, 8), 8), :]
        return [(eight[u : u + 1, :], eight[2 + u : 3 + u, :]) for u in range(2)]

    digits = []
    for other in (0, 1, 16, 17):
        digits += pieces(lax.bitwise_xor(ctx, other))
    row = [hi * 64.0 + lo for hi, lo in digits]
    col = [jnp.broadcast_to(r, (128, 128)).T for r in row]
    at_row = rows((128, 128)).astype(F32)
    for b in range(8):
        below = jnp.zeros((128, 128), F32)
        for a in range(8):
            below = below + jnp.where(col[a] < row[b], 1.0, 0.0)
        rank = jnp.sum(below, axis=0, keepdims=True)
        for a in range(8):
            perm[a * 128 : (a + 1) * 128, b * 128 : (b + 1) * 128] = jnp.where(
                at_row + float(a * 128) == rank, 1.0, 0.0
            ).astype(BF)
    line = rows((16, 1024))
    high = jnp.concatenate([hi for hi, _ in digits], axis=1)
    low = jnp.concatenate([lo for _, lo in digits], axis=1)
    both = jnp.where(line == 0, high, jnp.where(line == 1, low, 0.0)).astype(BF)
    both = lax.dot_general(
        both, perm[...], (((1,), (1,)), ((), ())), preferred_element_type=F32
    )
    ordered = both[0:1] * 64.0 + both[1:2]
    line = rows((8, 128))
    lane = lanes((8, 128))
    most = jnp.zeros((8, 128), F32)
    for c in range(8):
        posk[c : c + 1, :] = ordered[:, c * 128 : (c + 1) * 128]
    for t in range(TILES):
        tile = ordered[:, t * 256 : (t + 1) * 256]
        posq[t * 8 : (t + 1) * 8, :] = jnp.broadcast_to(
            jnp.concatenate([tile] * 4, axis=1), (8, WIDE)
        )
        top = jnp.max(tile[:, 128:], axis=1, keepdims=True)
        most = jnp.where(line == t, jnp.broadcast_to(top, (8, 128)), most)
    result = jnp.zeros((8, 128), F32)
    for z in range(8):
        some = jnp.zeros((8, 128), F32)
        for other in (0, 1, 16, 17):
            for hi, lo in pieces(z * 2 + other):
                some = some + jnp.where(hi * 64.0 + lo <= most, 1.0, 0.0)
        result = jnp.where(lane == z, jnp.sum(some, axis=1, keepdims=True), result)
    counts[...] = result.astype(jnp.int32)


def project(place, tokens, weights, s):
    dp = place[0]
    y_lo, x = lax.div(dp, 4), lax.rem(dp, 4)
    total = None
    for n, block in enumerate(weights):
        other = lax.rem(x + (0, 3, 1, 2)[n % 4], 4)
        owner = (y_lo if n < 4 else 1 - y_lo) * 4 + other
        part = tokens[s][:, pl.ds(pl.multiple_of(owner * 256, 256), 256)]
        term = dot(part, block[...])
        total = term if total is None else total + term
    return total.astype(BF)


def project_kernel(place, perm, posk, t0, t1, t2, t3, *refs):
    weights = refs[:8]
    out, queries, held = refs[8:]
    for s in range(4):
        held[s * 256 : (s + 1) * 256, :] = project(place, (t0, t1, t2, t3), weights, s)
    low = lanes((256, 128)) < 64
    p = posk[...]
    high = jnp.floor(p * (1.0 / 64.0))
    rest = p - high * 64.0
    none = jnp.zeros((4, 128), F32)
    kept = None
    for t in range(TILES):
        u = t // 2
        at = u * HALF
        ordered = dot(perm[t * 256 : (t + 1) * 256, :], held[...])
        kv = ordered[:, 256:]
        if t % 2 == 0:
            kept = kv
        else:
            out[at : at + 256, :] = jnp.where(low, kept, pltpu.roll(kv, 64, 1)).astype(BF)
        for i in range(2):
            c = (t % 2) * 2 + i
            out[at + 256 + c * 64 : at + 320 + c * 64, :] = kv[
                i * 128 : (i + 1) * 128
            ].T[64:].astype(BF)
            for j in range(2):
                q = ordered[i * 128 : (i + 1) * 128, j * 128 : (j + 1) * 128].T * 0.125
                for e in range(2):
                    lane = (j * 2 + e) * 256 + i * 128
                    queries[t * 64 : (t + 1) * 64, lane : lane + 128] = q[
                        e * 64 : (e + 1) * 64
                    ].astype(BF)
    for u in range(2):
        digits = jnp.concatenate(
            [high[u * 4 : u * 4 + 4], none, rest[u * 4 : u * 4 + 4], none], axis=0
        )
        out[u * HALF + 512 : (u + 1) * HALF, :] = digits.astype(BF)


def attend_kernel(blocks, first, last, *refs):
    refs = list(refs)
    place, counts, q, posq = refs[:4]
    del refs[:4]
    n_refs = 1 + max(n for _, halves in blocks for n, _ in halves)
    held = refs[:n_refs]
    del refs[:n_refs]
    if not first:
        m_in, acc_in = refs[:2]
        del refs[:2]
    if last:
        perm = refs.pop(0)
        outs = refs[:4]
        del refs[:4]
        kk, v1, pk, scores, mixed = refs
    else:
        m_ref, acc_ref, kk, v1, pk, scores = refs
    lines = []
    n = 0
    for _, halves in blocks:
        for ref, at in halves:
            a = held[ref][at : at + 256, :].astype(F32)
            b = pltpu.roll(a, 64, 1)
            kk[n * 512 : n * 512 + 256, :] = a.astype(BF)
            kk[n * 512 + 256 : n * 512 + 512, :] = b.astype(BF)
            for c in range(4):
                v1[0:64, n * 512 + c * 128 : n * 512 + (c + 1) * 128] = held[ref][
                    at + 256 + c * 64 : at + 320 + c * 64, :
                ]
            digits = held[ref][at + 512 : at + HALF, :].astype(F32)
            lines.append(digits[0:8] * 64.0 + digits[8:16])
            n += 1
    v1[64:80, :] = jnp.ones((16, n * 512), BF)
    lines.append(jnp.zeros((128 - 8 * n, 128), F32))
    columns = jnp.concatenate(lines, axis=0).T
    for i in range(n):
        for c in range(4):
            k = i * 4 + c
            pk[k * 128 : (k + 1) * 128, :] = jnp.broadcast_to(
                columns[:, i * 8 + c : i * 8 + c + 1], (128, 128)
            )
    z = lax.rem(lax.div(place[1], 2), 8)

    def tile_step(t, _):
        qt = q[pl.ds(pl.multiple_of(t * 64, 64), 64), :]
        pq = posq[pl.ds(pl.multiple_of(t * 8, 8), 8), :][0:1]
        m_at = pl.ds(pl.multiple_of(t * 8, 8), 8)
        acc_at = pl.ds(pl.multiple_of(t * 80, 16), 80)
        if first:
            m = jnp.full((1, WIDE), -1e29, F32)
            acc = jnp.zeros((80, WIDE), F32)
        else:
            m = m_in[m_at, :][0:1]
            acc = acc_in[acc_at, :]

        def some(base, steps, state):
            m, acc = state
            high = m
            for j in range(steps):
                at = base + j * KEYS
                s = dot(kk[at : at + KEYS, 0:64], qt)
                line = jnp.concatenate([pk[at : at + KEYS, :]] * (WIDE // 128), axis=1)
                s = jnp.where(line <= pq, s, -1e30)
                scores[j] = s
                high = jnp.maximum(high, jnp.max(s, axis=0, keepdims=True))
            acc = acc * jnp.exp(m - high)
            for j in range(steps):
                at = base + j * KEYS
                p = jnp.exp(scores[j] - high).astype(BF)
                acc = acc + dot(v1[:, at : at + KEYS], p)
            return high, acc

        state = (m, acc)
        for i, (away, _) in enumerate(blocks):
            other = lax.rem(z + away + 8, 8)
            steps = lax.div(counts[t, other] + (KEYS - 1), KEYS)
            branches = [functools.partial(some, i * 1024, k) for k in range(1024 // KEYS + 1)]
            branches[0] = lambda state: state
            state = lax.switch(steps, branches, state)
        m, acc = state
        if last:
            o = acc[0:64] / acc[64:65]
            for h in range(4):
                mixed[h * 64 : (h + 1) * 64, pl.ds(pl.multiple_of(t * 256, 256), 256)] = o[
                    :, h * 256 : (h + 1) * 256
                ].astype(BF)
        else:
            m_ref[m_at, :] = jnp.broadcast_to(m, (8, WIDE))
            acc_ref[acc_at, :] = acc
        return 0

    lax.fori_loop(0, TILES, tile_step, 0)
    if last:
        for s in range(4):
            back = dot(mixed[...], perm[:, s * 256 : (s + 1) * 256])
            outs[s][...] = back.T.astype(BF)


def out_kernel(half, last, *refs):
    place, a0, a1, w_own, w_core = refs[:5]
    dp = place[0]
    y_lo, x = lax.div(dp, 4), lax.rem(dp, 4)
    out = refs[-1]
    for n, step in enumerate((0, 3, 1, 2)):
        other = lax.rem(x + step, 4)
        for r in range(2):
            owner = (y_lo if r == 0 else 1 - y_lo) * 4 + other
            to = pl.ds(pl.multiple_of(owner * 256, 256), 256)
            at = n * 1024 + r * 512 + half * 256
            total = refs[5][:, to] if last else None
            for a, w in ((a0, w_own), (a1, w_core)):
                term = lax.dot_general(
                    a[...], w[at : at + 256, :], (((1,), (1,)), ((), ())), preferred_element_type=F32
                )
                total = term if total is None else total + term
            out[:, to] = total.astype(out.dtype)


def after(value, other):
    return lax.optimization_barrier((value, other))[0]


def spread(pair):
    return pair, send(pair, X_UP), send(pair, X_DOWN), send(pair, X_FAR)


def attend(place, counts, q, posq, held, blocks, state, perm=None):
    first, last = state is None, perm is not None
    args = [place, counts, q, posq, *held]
    specs = [SMEM, SMEM] + [VMEM] * (2 + len(held))
    aliases = {}
    if not first:
        if not last:
            aliases = {len(args): 0, len(args) + 1: 1}
        args += state
        specs += [VMEM] * 2
    n = len(blocks)
    scratch = [
        pltpu.VMEM((n * 1024, 128), BF),
        pltpu.VMEM((80, n * 1024), BF),
        pltpu.VMEM((n * 1024, 128), F32),
        pltpu.VMEM((1024 // KEYS, KEYS, WIDE), F32),
    ]
    if last:
        args.append(perm)
        specs.append(VMEM)
        out = [jax.ShapeDtypeStruct((256, 256), BF)] * 4
        scratch.append(pltpu.VMEM((256, 1024), BF))
    else:
        out = [
            jax.ShapeDtypeStruct((TILES * 8, WIDE), F32),
            jax.ShapeDtypeStruct((TILES * 80, WIDE), F32),
        ]
    return call(
        functools.partial(attend_kernel, blocks, first, last),
        out,
        args,
        specs,
        flops=n * 4096 * 1024 * 64 * 8,
        scratch=scratch,
        aliases=aliases,
    )


def body(master, moment1, moment2, gradient, tokens, gain, positions):
    place = jnp.stack([lax.axis_index("dp"), lax.axis_index("ctx")]).astype(jnp.int32)
    shard = jax.ShapeDtypeStruct(master.shape, F32)
    slot = jax.ShapeDtypeStruct((8, 768), F32)
    new_master, new_moment1, new_moment2, *sent = call(
        adam_kernel,
        [shard, shard, shard, slot, slot, slot, slot],
        [place, master, moment1, moment2, gradient, positions],
        [SMEM] + [HBM] * 5,
        scratch=[
            pltpu.VMEM((4, 8, 2560), F32),
            pltpu.VMEM((1, 256), jnp.int32),
            pltpu.SemaphoreType.DMA((5,)),
        ],
    )
    group = [sent[0], send(sent[1], CORE), send(sent[2], Y_HI), send(sent[3], DIAG)]
    normed = call(
        norm_kernel,
        jax.ShapeDtypeStruct((256, 2048), BF),
        [tokens.reshape(256, 2048), gain.reshape(1, 2048), sent[0]],
        [VMEM] * 2 + [pl.BlockSpec(memory_space=pl.ANY)],
    )
    by_y = send(after(normed, group), Y_HI)
    by_core = send(normed, CORE)
    mixed = call(
        repeat_kernel,
        jax.ShapeDtypeStruct((256, 768), BF),
        [*group, normed],
        [VMEM] * 4 + [pl.BlockSpec(memory_space=pl.ANY)],
    )
    along_z = [[y * 16 + z * 2 + c for z in range(8)] for y in range(2) for c in range(2)]
    mixed = lax.all_to_all(mixed, "ctx", 0, 0, tiled=True, axis_index_groups=along_z)
    mine_qkv, mine_out, posd = call(
        place_kernel,
        [
            jax.ShapeDtypeStruct((256, 384), BF),
            jax.ShapeDtypeStruct((256, 256), BF),
            jax.ShapeDtypeStruct((256, 128), F32),
        ],
        [place, mixed],
        [SMEM, VMEM],
    )
    perm, posq, posk, counts = call(
        order_kernel,
        [
            jax.ShapeDtypeStruct((1024, 1024), BF),
            jax.ShapeDtypeStruct((TILES * 8, WIDE), F32),
            jax.ShapeDtypeStruct((8, 128), F32),
            jax.ShapeDtypeStruct((8, 128), jnp.int32),
        ],
        [place, posd],
        [SMEM, VMEM],
    )
    near = send(mine_qkv, Y_LO)
    own = spread(mine_qkv)
    slots = [normed, by_core, by_y, send(after(by_y, (own, near, counts)), CORE)]
    weights = own + spread(after(near, counts))
    block, q = call(
        project_kernel,
        [
            jax.ShapeDtypeStruct((2 * HALF, 128), BF),
            jax.ShapeDtypeStruct((TILES * 64, WIDE), BF),
        ],
        [place, perm, posk, *slots, *weights],
        [SMEM] + [VMEM] * 14,
        flops=2 * 1024 * 3072 * 384,
        scratch=[pltpu.VMEM((1024, 384), BF)],
    )
    mine_out = after(mine_out, weights[1])
    out_pair = jnp.concatenate([mine_out, send(mine_out, Y_HI)], axis=0)
    out_pair = jnp.concatenate([out_pair, send(out_pair, Y_LO)], axis=0)

    def whole(ref):
        return ((ref, 0), (ref, HALF))

    state = attend(place, counts, q, posq, [block], [(0, whole(0))], None)
    up, down = block, block
    for step in range(1, 4):
        up, down = send(up, Z_UP), send(down, Z_DOWN)
        if step == 1:
            out_own = jnp.concatenate(spread(after(out_pair, (up, down, state[0]))), axis=0)
        state = attend(
            place, counts, q, posq, [up, down], [(-step, whole(0)), (step, whole(1))], state
        )
    far = [send(up[:HALF], Z_UP), send(down[HALF:], Z_DOWN)]
    out_core = send(after(out_own, (far, state[0])), CORE)
    parts = attend(place, counts, q, posq, far, [(4, ((0, 0), (1, 0)))], state, perm)
    by_y, by_both, by_core = send(parts[2], Y_HI), send(parts[3], DIAG), send(parts[1], CORE)
    flops = 256 * 1024 * 2048
    half = call(
        functools.partial(out_kernel, 0, False),
        jax.ShapeDtypeStruct((256, 2048), F32),
        [place, parts[0], by_core, out_own, out_core],
        [SMEM] + [VMEM] * 4,
        flops=flops,
    )
    block_out = call(
        functools.partial(out_kernel, 1, True),
        jax.ShapeDtypeStruct((256, 2048), BF),
        [place, by_y, by_both, out_own, out_core, half],
        [SMEM] + [VMEM] * 5,
        flops=flops,
    )
    return new_master, new_moment1, new_moment2, block_out.reshape(1, 256, 2048)


def solution(mesh):
    rows_split = P(AXES, None)
    return jax.shard_map(
        body,
        mesh=mesh,
        in_specs=(
            rows_split,
            rows_split,
            rows_split,
            rows_split,
            P("dp", "ctx", None),
            P(),
            P("dp", "ctx"),
        ),
        out_specs=(rows_split, rows_split, rows_split, P("dp", "ctx", None)),
        check_vma=False,
    )
```

```python
import functools

import jax
import jax.numpy as jnp
from jax import lax
from jax.experimental import pallas as pl
from jax.experimental.pallas import tpu as pltpu
from jax.sharding import PartitionSpec as P

STEP = 100
beta_one = 0.9
beta_two = 0.95
learn_rate = 0.002
decay_rate = 0.1
epsilon = 1e-08

AXES = ("dp", "ctx")
BF = jnp.bfloat16
F32 = jnp.float32
MIB = 1 << 20
HALF = 528
TILES = 4
WIDE = 1024
KEYS = 256


def device_of(x, y, z, core):
    x, y, z = x % 4, y % 4, z % 8
    return ((y % 2) * 4 + x) * 32 + (y // 2) * 16 + z * 2 + core


def moved(target):
    return [
        (device_of(x, y, z, c), device_of(*target(x, y, z, c)))
        for x in range(4)
        for y in range(4)
        for z in range(8)
        for c in range(2)
    ]


CORE = moved(lambda x, y, z, c: (x, y, z, 1 - c))
Y_HI = moved(lambda x, y, z, c: (x, y + 2, z, c))
DIAG = moved(lambda x, y, z, c: (x, y + 2, z, 1 - c))
Y_LO = moved(lambda x, y, z, c: (x, y ^ 1, z, c))
X_UP = moved(lambda x, y, z, c: (x + 1, y, z, c))
X_DOWN = moved(lambda x, y, z, c: (x - 1, y, z, c))
X_FAR = moved(lambda x, y, z, c: (x + 2, y, z, c))
Z_UP = moved(lambda x, y, z, c: (x, y, z + 1, c))
Z_DOWN = moved(lambda x, y, z, c: (x, y, z - 1, c))


def send(value, perm):
    return lax.ppermute(value, AXES, perm)


VMEM = pl.BlockSpec(memory_space=pltpu.VMEM)
SMEM = pl.BlockSpec(memory_space=pltpu.SMEM)
HBM = pl.BlockSpec(memory_space=pltpu.HBM)


def call(kernel, out, args, specs, limit=32, flops=0, scratch=(), aliases=None):
    moved_bytes = sum(a.size * a.dtype.itemsize for a in args)
    return pl.pallas_call(
        kernel,
        out_shape=out,
        in_specs=specs,
        out_specs=jax.tree.map(lambda _: VMEM, out),
        scratch_shapes=list(scratch),
        input_output_aliases=aliases or {},
        cost_estimate=pl.CostEstimate(
            flops=flops, bytes_accessed=moved_bytes, transcendentals=0
        ),
        compiler_params=pltpu.CompilerParams(vmem_limit_bytes=limit * MIB),
    )(*args)


def lanes(shape):
    return lax.broadcasted_iota(jnp.int32, shape, len(shape) - 1)


def rows(shape):
    return lax.broadcasted_iota(jnp.int32, shape, len(shape) - 2)


def dot(a, b):
    return jnp.dot(a, b, preferred_element_type=F32)


def norm_kernel(tokens, gain, sent, normed, held, scale, sems):
    del sent
    first = pltpu.make_async_copy(gain, scale, sems.at[4])
    first.start()
    copies = [
        pltpu.make_async_copy(
            tokens.at[r * 64 : (r + 1) * 64], held.at[r * 64 : (r + 1) * 64], sems.at[r]
        )
        for r in range(4)
    ]
    for copy in copies:
        copy.start()
    first.wait()
    for r in range(4):
        copies[r].wait()
        wide = held[r * 64 : (r + 1) * 64, :].astype(F32)
        meansq = jnp.mean(wide * wide, axis=1, keepdims=True)
        normed[r * 64 : (r + 1) * 64, :] = (
            wide * lax.rsqrt(meansq + 1e-05) * scale[...]
        ).astype(BF)


def adam_kernel(
    place,
    master_hbm,
    moment1_hbm,
    moment2_hbm,
    gradient_hbm,
    pos_hbm,
    nm,
    n1,
    n2,
    s0,
    s1,
    s2,
    s3,
    held,
    pos,
    sems,
):
    copies = [
        pltpu.make_async_copy(ref, held.at[i], sems.at[i])
        for i, ref in enumerate((master_hbm, moment1_hbm, moment2_hbm, gradient_hbm))
    ]
    copies.append(pltpu.make_async_copy(pos_hbm, pos, sems.at[4]))
    for copy in copies:
        copy.start()
    for copy in copies:
        copy.wait()
    g = held[3]
    m1 = beta_one * held[1] + (1.0 - beta_one) * g
    m2 = beta_two * held[2] + (1.0 - beta_two) * g * g
    update = m1 / (1.0 - beta_one**STEP) / (jnp.sqrt(m2 / (1.0 - beta_two**STEP)) + epsilon)
    old = held[0]
    new = old - learn_rate * (update + decay_rate * old)
    nm[...] = new
    n1[...] = m1
    n2[...] = m2
    low = lanes((8, 128)) < 64
    line = rows((8, 128))
    digits = jnp.zeros((8, 128), F32)
    for u in range(2):
        p = pos[:, u * 128 : (u + 1) * 128]
        hi = lax.shift_right_logical(p, 6).astype(F32)
        lo = lax.bitwise_and(p, 63).astype(F32)
        digits = jnp.where(line == u, hi, jnp.where(line == 2 + u, lo, digits))
    rounded = new.astype(BF).astype(F32)
    parts = []
    for h in range(4):
        at = (h // 2) * 128
        kt = rounded[:, 1024 + at : 1152 + at]
        vt = rounded[:, 1280 + at : 1408 + at]
        if h % 2 == 0:
            kv = jnp.where(low, kt, pltpu.roll(vt, 64, 1))
        else:
            kv = jnp.where(low, pltpu.roll(kt, 64, 1), vt)
        parts.append(
            jnp.concatenate(
                [
                    rounded[:, h * 256 : (h + 1) * 256],
                    kv,
                    rounded[:, 1536 + h * 256 : 1792 + h * 256],
                    digits,
                ],
                axis=1,
            )
        )
    ctx = place[1]
    mine = lax.div(ctx, 16) * 2 + lax.rem(ctx, 2)
    for s, ref in enumerate((s0, s1, s2, s3)):
        h = lax.bitwise_xor(mine, s)
        lower = jnp.where(h == 0, parts[0], parts[1])
        upper = jnp.where(h == 2, parts[2], parts[3])
        ref[...] = jnp.where(h < 2, lower, upper)


def repeat_kernel(r0, r1, r2, r3, out):
    block = jnp.concatenate([r0[...], r1[...], r2[...], r3[...]], axis=0).astype(BF)
    for z in range(8):
        out[z * 32 : (z + 1) * 32, :] = block


def place_kernel(place, mixed, qkv, out, posd):
    ctx = place[1]
    y_hi, core = lax.div(ctx, 16), lax.rem(ctx, 2)
    i = rows((256, 256))
    j = lax.shift_right_logical(i, 3)
    slot = lax.bitwise_xor(lax.shift_right_logical(j, 4), y_hi) * 2 + lax.bitwise_xor(
        lax.bitwise_and(j, 1), core
    )
    z = lax.bitwise_and(lax.shift_right_logical(j, 1), 7)
    source = z * 32 + slot * 8 + lax.bitwise_and(i, 7)
    pick = jnp.where(lanes((256, 256)) == source, 1.0, 0.0).astype(BF)
    result = dot(pick, mixed[...])
    qkv[...] = result[:, :384].astype(BF)
    out[...] = result[:, 384:640].astype(BF)
    posd[...] = result[:, 640:]


def order_kernel(place, posd, perm, posq, posk, counts):
    ctx = place[1]

    def pieces(j):
        eight = posd[pl.ds(pl.multiple_of(j * 8, 8), 8), :]
        return [(eight[u : u + 1, :], eight[2 + u : 3 + u, :]) for u in range(2)]

    digits = []
    for other in (0, 1, 16, 17):
        digits += pieces(lax.bitwise_xor(ctx, other))
    row = [hi * 64.0 + lo for hi, lo in digits]
    col = [jnp.broadcast_to(r, (128, 128)).T for r in row]
    at_row = rows((128, 128)).astype(F32)
    for b in range(8):
        below = jnp.zeros((128, 128), F32)
        for a in range(8):
            below = below + jnp.where(col[a] < row[b], 1.0, 0.0)
        rank = jnp.sum(below, axis=0, keepdims=True)
        for a in range(8):
            perm[a * 128 : (a + 1) * 128, b * 128 : (b + 1) * 128] = jnp.where(
                at_row + float(a * 128) == rank, 1.0, 0.0
            ).astype(BF)
    line = rows((16, 1024))
    high = jnp.concatenate([hi for hi, _ in digits], axis=1)
    low = jnp.concatenate([lo for _, lo in digits], axis=1)
    both = jnp.where(line == 0, high, jnp.where(line == 1, low, 0.0)).astype(BF)
    both = lax.dot_general(
        both, perm[...], (((1,), (1,)), ((), ())), preferred_element_type=F32
    )
    ordered = both[0:1] * 64.0 + both[1:2]
    line = rows((8, 128))
    lane = lanes((8, 128))
    most = jnp.zeros((8, 128), F32)
    for c in range(8):
        posk[c : c + 1, :] = ordered[:, c * 128 : (c + 1) * 128]
    for t in range(TILES):
        tile = ordered[:, t * 256 : (t + 1) * 256]
        posq[t * 8 : (t + 1) * 8, :] = jnp.broadcast_to(
            jnp.concatenate([tile] * 4, axis=1), (8, WIDE)
        )
        top = jnp.max(tile[:, 128:], axis=1, keepdims=True)
        most = jnp.where(line == t, jnp.broadcast_to(top, (8, 128)), most)
    result = jnp.zeros((8, 128), F32)
    for z in range(8):
        some = jnp.zeros((8, 128), F32)
        for other in (0, 1, 16, 17):
            for hi, lo in pieces(z * 2 + other):
                some = some + jnp.where(hi * 64.0 + lo <= most, 1.0, 0.0)
        result = jnp.where(lane == z, jnp.sum(some, axis=1, keepdims=True), result)
    counts[...] = result.astype(jnp.int32)


def project(place, tokens, weights, s):
    dp = place[0]
    y_lo, x = lax.div(dp, 4), lax.rem(dp, 4)
    total = None
    for n, block in enumerate(weights):
        other = lax.rem(x + (0, 3, 1, 2)[n % 4], 4)
        owner = (y_lo if n < 4 else 1 - y_lo) * 4 + other
        part = tokens[s][:, pl.ds(pl.multiple_of(owner * 256, 256), 256)]
        term = dot(part, block[...])
        total = term if total is None else total + term
    return total.astype(BF)


def project_kernel(place, perm, posk, t0, t1, t2, t3, *refs):
    weights = refs[:8]
    out, queries, held = refs[8:]
    for s in range(4):
        held[s * 256 : (s + 1) * 256, :] = project(place, (t0, t1, t2, t3), weights, s)
    low = lanes((256, 128)) < 64
    p = posk[...]
    high = jnp.floor(p * (1.0 / 64.0))
    rest = p - high * 64.0
    none = jnp.zeros((4, 128), F32)
    kept = None
    for t in range(TILES):
        u = t // 2
        at = u * HALF
        ordered = dot(perm[t * 256 : (t + 1) * 256, :], held[...])
        kv = ordered[:, 256:]
        if t % 2 == 0:
            kept = kv
        else:
            out[at : at + 256, :] = jnp.where(low, kept, pltpu.roll(kv, 64, 1)).astype(BF)
        for i in range(2):
            c = (t % 2) * 2 + i
            out[at + 256 + c * 64 : at + 320 + c * 64, :] = kv[
                i * 128 : (i + 1) * 128
            ].T[64:].astype(BF)
            for j in range(2):
                q = ordered[i * 128 : (i + 1) * 128, j * 128 : (j + 1) * 128].T * 0.125
                for e in range(2):
                    lane = (j * 2 + e) * 256 + i * 128
                    queries[t * 64 : (t + 1) * 64, lane : lane + 128] = q[
                        e * 64 : (e + 1) * 64
                    ].astype(BF)
    for u in range(2):
        digits = jnp.concatenate(
            [high[u * 4 : u * 4 + 4], none, rest[u * 4 : u * 4 + 4], none], axis=0
        )
        out[u * HALF + 512 : (u + 1) * HALF, :] = digits.astype(BF)


def attend_kernel(blocks, first, last, *refs):
    refs = list(refs)
    place, counts, q, posq = refs[:4]
    del refs[:4]
    n_refs = 1 + max(n for _, halves in blocks for n, _ in halves)
    held = refs[:n_refs]
    del refs[:n_refs]
    if not first:
        m_in, acc_in = refs[:2]
        del refs[:2]
    if last:
        perm = refs.pop(0)
        outs = refs[:4]
        del refs[:4]
        kk, v1, pk, scores, mixed = refs
    else:
        m_ref, acc_ref, kk, v1, pk, scores = refs
    lines = []
    n = 0
    for _, halves in blocks:
        for ref, at in halves:
            a = held[ref][at : at + 256, :].astype(F32)
            b = pltpu.roll(a, 64, 1)
            kk[n * 512 : n * 512 + 256, :] = a.astype(BF)
            kk[n * 512 + 256 : n * 512 + 512, :] = b.astype(BF)
            for c in range(4):
                v1[0:64, n * 512 + c * 128 : n * 512 + (c + 1) * 128] = held[ref][
                    at + 256 + c * 64 : at + 320 + c * 64, :
                ]
            digits = held[ref][at + 512 : at + HALF, :].astype(F32)
            lines.append(digits[0:8] * 64.0 + digits[8:16])
            n += 1
    v1[64:80, :] = jnp.ones((16, n * 512), BF)
    lines.append(jnp.zeros((128 - 8 * n, 128), F32))
    columns = jnp.concatenate(lines, axis=0).T
    for i in range(n):
        for c in range(4):
            k = i * 4 + c
            pk[k * 128 : (k + 1) * 128, :] = jnp.broadcast_to(
                columns[:, i * 8 + c : i * 8 + c + 1], (128, 128)
            )
    z = lax.rem(lax.div(place[1], 2), 8)

    def tile_step(t, _):
        qt = q[pl.ds(pl.multiple_of(t * 64, 64), 64), :]
        pq = posq[pl.ds(pl.multiple_of(t * 8, 8), 8), :][0:1]
        m_at = pl.ds(pl.multiple_of(t * 8, 8), 8)
        acc_at = pl.ds(pl.multiple_of(t * 80, 16), 80)
        if first:
            m = jnp.full((1, WIDE), -1e29, F32)
            acc = jnp.zeros((80, WIDE), F32)
        else:
            m = m_in[m_at, :][0:1]
            acc = acc_in[acc_at, :]

        def some(base, steps, state):
            m, acc = state
            high = m
            chunks = [(j * KEYS, KEYS) for j in range(steps // 2)]
            if steps % 2:
                chunks.append((steps // 2 * KEYS, KEYS // 2))
            for off, size in chunks:
                at = base + off
                s = dot(kk[at : at + size, 0:64], qt)
                line = jnp.concatenate([pk[at : at + size, :]] * (WIDE // 128), axis=1)
                s = jnp.where(line <= pq, s, -1e30)
                scores[off : off + size, :] = s
                high = jnp.maximum(high, jnp.max(s, axis=0, keepdims=True))
            acc = acc * jnp.exp(m - high)
            for off, size in chunks:
                at = base + off
                p = jnp.exp(scores[off : off + size, :] - high).astype(BF)
                acc = acc + dot(v1[:, at : at + size], p)
            return high, acc

        state = (m, acc)
        for i, (away, _) in enumerate(blocks):
            other = lax.rem(z + away + 8, 8)
            half = KEYS // 2
            steps = lax.div(counts[t, other] + (half - 1), half)
            branches = [functools.partial(some, i * 1024, k) for k in range(1024 // half + 1)]
            branches[0] = lambda state: state
            state = lax.switch(steps, branches, state)
        m, acc = state
        if last:
            o = acc[0:64] / acc[64:65]
            for h in range(4):
                mixed[h * 64 : (h + 1) * 64, pl.ds(pl.multiple_of(t * 256, 256), 256)] = o[
                    :, h * 256 : (h + 1) * 256
                ].astype(BF)
        else:
            m_ref[m_at, :] = jnp.broadcast_to(m, (8, WIDE))
            acc_ref[acc_at, :] = acc
        return 0

    lax.fori_loop(0, TILES, tile_step, 0)
    if last:
        for s in range(4):
            back = dot(mixed[...], perm[:, s * 256 : (s + 1) * 256])
            outs[s][...] = back.T.astype(BF)


def out_kernel(half, last, *refs):
    place, a0, a1, w_own, w_core = refs[:5]
    dp = place[0]
    y_lo, x = lax.div(dp, 4), lax.rem(dp, 4)
    out = refs[-1]
    for n, step in enumerate((0, 3, 1, 2)):
        other = lax.rem(x + step, 4)
        for r in range(2):
            owner = (y_lo if r == 0 else 1 - y_lo) * 4 + other
            to = pl.ds(pl.multiple_of(owner * 256, 256), 256)
            at = n * 1024 + r * 512 + half * 256
            total = refs[5][:, to] if last else None
            for a, w in ((a0, w_own), (a1, w_core)):
                term = lax.dot_general(
                    a[...], w[at : at + 256, :], (((1,), (1,)), ((), ())), preferred_element_type=F32
                )
                total = term if total is None else total + term
            out[:, to] = total.astype(out.dtype)


def after(value, other):
    return lax.optimization_barrier((value, other))[0]


def spread(pair):
    return pair, send(pair, X_UP), send(pair, X_DOWN), send(pair, X_FAR)


def attend(place, counts, q, posq, held, blocks, state, perm=None):
    first, last = state is None, perm is not None
    args = [place, counts, q, posq, *held]
    specs = [SMEM, SMEM] + [VMEM] * (2 + len(held))
    aliases = {}
    if not first:
        if not last:
            aliases = {len(args): 0, len(args) + 1: 1}
        args += state
        specs += [VMEM] * 2
    n = len(blocks)
    scratch = [
        pltpu.VMEM((n * 1024, 128), BF),
        pltpu.VMEM((80, n * 1024), BF),
        pltpu.VMEM((n * 1024, 128), F32),
        pltpu.VMEM((1024, WIDE), F32),
    ]
    if last:
        args.append(perm)
        specs.append(VMEM)
        out = [jax.ShapeDtypeStruct((256, 256), BF)] * 4
        scratch.append(pltpu.VMEM((256, 1024), BF))
    else:
        out = [
            jax.ShapeDtypeStruct((TILES * 8, WIDE), F32),
            jax.ShapeDtypeStruct((TILES * 80, WIDE), F32),
        ]
    return call(
        functools.partial(attend_kernel, blocks, first, last),
        out,
        args,
        specs,
        flops=n * 4096 * 1024 * 64 * 8,
        scratch=scratch,
        aliases=aliases,
    )


def body(master, moment1, moment2, gradient, tokens, gain, positions):
    place = jnp.stack([lax.axis_index("dp"), lax.axis_index("ctx")]).astype(jnp.int32)
    shard = jax.ShapeDtypeStruct(master.shape, F32)
    slot = jax.ShapeDtypeStruct((8, 768), F32)
    new_master, new_moment1, new_moment2, *sent = call(
        adam_kernel,
        [shard, shard, shard, slot, slot, slot, slot],
        [place, master, moment1, moment2, gradient, positions],
        [SMEM] + [HBM] * 5,
        limit=60,
        scratch=[
            pltpu.VMEM((4, 8, 2560), F32),
            pltpu.VMEM((1, 256), jnp.int32),
            pltpu.SemaphoreType.DMA((5,)),
        ],
    )
    group = [sent[0], send(sent[1], CORE), send(sent[2], Y_HI), send(sent[3], DIAG)]
    normed = call(
        norm_kernel,
        jax.ShapeDtypeStruct((256, 2048), BF),
        [tokens.reshape(256, 2048), gain.reshape(1, 2048), sent[0]],
        [HBM] * 2 + [pl.BlockSpec(memory_space=pl.ANY)],
        limit=60,
        scratch=[
            pltpu.VMEM((256, 2048), BF),
            pltpu.VMEM((1, 2048), F32),
            pltpu.SemaphoreType.DMA((5,)),
        ],
    )
    by_y = send(after(normed, group), Y_HI)
    by_core = send(normed, CORE)
    mixed = call(
        repeat_kernel,
        jax.ShapeDtypeStruct((256, 768), BF),
        group,
        [VMEM] * 4,
    )
    along_z = [[y * 16 + z * 2 + c for z in range(8)] for y in range(2) for c in range(2)]
    mixed = lax.all_to_all(mixed, "ctx", 0, 0, tiled=True, axis_index_groups=along_z)
    mine_qkv, mine_out, posd = call(
        place_kernel,
        [
            jax.ShapeDtypeStruct((256, 384), BF),
            jax.ShapeDtypeStruct((256, 256), BF),
            jax.ShapeDtypeStruct((256, 128), F32),
        ],
        [place, mixed],
        [SMEM, VMEM],
    )
    perm, posq, posk, counts = call(
        order_kernel,
        [
            jax.ShapeDtypeStruct((1024, 1024), BF),
            jax.ShapeDtypeStruct((TILES * 8, WIDE), F32),
            jax.ShapeDtypeStruct((8, 128), F32),
            jax.ShapeDtypeStruct((8, 128), jnp.int32),
        ],
        [place, posd],
        [SMEM, VMEM],
    )
    near = send(mine_qkv, Y_LO)
    own = spread(mine_qkv)
    slots = [normed, by_core, by_y, send(after(by_y, (own, near, counts)), CORE)]
    weights = own + spread(after(near, counts))
    block, q = call(
        project_kernel,
        [
            jax.ShapeDtypeStruct((2 * HALF, 128), BF),
            jax.ShapeDtypeStruct((TILES * 64, WIDE), BF),
        ],
        [place, perm, posk, *slots, *weights],
        [SMEM] + [VMEM] * 14,
        flops=2 * 1024 * 3072 * 384,
        scratch=[pltpu.VMEM((1024, 384), BF)],
    )
    mine_out = after(mine_out, weights[1])
    out_pair = jnp.concatenate([mine_out, send(mine_out, Y_HI)], axis=0)
    out_pair = jnp.concatenate([out_pair, send(out_pair, Y_LO)], axis=0)

    def whole(ref):
        return ((ref, 0), (ref, HALF))

    state = attend(place, counts, q, posq, [block], [(0, whole(0))], None)
    up, down = block, block
    for step in range(1, 4):
        up, down = send(up, Z_UP), send(down, Z_DOWN)
        if step == 1:
            out_own = jnp.concatenate(spread(after(out_pair, (up, down, state[0]))), axis=0)
        state = attend(
            place, counts, q, posq, [up, down], [(-step, whole(0)), (step, whole(1))], state
        )
    far = [send(up[:HALF], Z_UP), send(down[HALF:], Z_DOWN)]
    out_core = send(after(out_own, (far, state[0])), CORE)
    parts = attend(place, counts, q, posq, far, [(4, ((0, 0), (1, 0)))], state, perm)
    by_y, by_both, by_core = send(parts[2], Y_HI), send(parts[3], DIAG), send(parts[1], CORE)
    flops = 256 * 1024 * 2048
    half = call(
        functools.partial(out_kernel, 0, False),
        jax.ShapeDtypeStruct((256, 2048), F32),
        [place, parts[0], by_core, out_own, out_core],
        [SMEM] + [VMEM] * 4,
        flops=flops,
    )
    block_out = call(
        functools.partial(out_kernel, 1, True),
        jax.ShapeDtypeStruct((256, 2048), BF),
        [place, by_y, by_both, out_own, out_core, half],
        [SMEM] + [VMEM] * 5,
        flops=flops,
    )
    return new_master, new_moment1, new_moment2, block_out.reshape(1, 256, 2048)


def solution(mesh):
    rows_split = P(AXES, None)
    return jax.shard_map(
        body,
        mesh=mesh,
        in_specs=(
            rows_split,
            rows_split,
            rows_split,
            rows_split,
            P("dp", "ctx", None),
            P(),
            P("dp", "ctx"),
        ),
        out_specs=(rows_split, rows_split, rows_split, P("dp", "ctx", None)),
        check_vma=False,
    )
```

```python
import functools

import jax
import jax.numpy as jnp
from jax import lax
from jax.experimental import pallas as pl
from jax.experimental.pallas import tpu as pltpu
from jax.sharding import PartitionSpec as P

STEP = 100
beta_one = 0.9
beta_two = 0.95
learn_rate = 0.002
decay_rate = 0.1
epsilon = 1e-08

AXES = ("dp", "ctx")
BF = jnp.bfloat16
F32 = jnp.float32
MIB = 1 << 20
HALF = 528
TILES = 4
WIDE = 1024
KEYS = 256


def device_of(x, y, z, core):
    x, y, z = x % 4, y % 4, z % 8
    return ((y % 2) * 4 + x) * 32 + (y // 2) * 16 + z * 2 + core


def moved(target):
    return [
        (device_of(x, y, z, c), device_of(*target(x, y, z, c)))
        for x in range(4)
        for y in range(4)
        for z in range(8)
        for c in range(2)
    ]


CORE = moved(lambda x, y, z, c: (x, y, z, 1 - c))
Y_HI = moved(lambda x, y, z, c: (x, y + 2, z, c))
DIAG = moved(lambda x, y, z, c: (x, y + 2, z, 1 - c))
Y_LO = moved(lambda x, y, z, c: (x, y ^ 1, z, c))
X_UP = moved(lambda x, y, z, c: (x + 1, y, z, c))
X_DOWN = moved(lambda x, y, z, c: (x - 1, y, z, c))
X_FAR = moved(lambda x, y, z, c: (x + 2, y, z, c))
Z_UP = moved(lambda x, y, z, c: (x, y, z + 1, c))
Z_DOWN = moved(lambda x, y, z, c: (x, y, z - 1, c))


def send(value, perm):
    return lax.ppermute(value, AXES, perm)


VMEM = pl.BlockSpec(memory_space=pltpu.VMEM)
SMEM = pl.BlockSpec(memory_space=pltpu.SMEM)
HBM = pl.BlockSpec(memory_space=pltpu.HBM)


def call(kernel, out, args, specs, limit=32, flops=0, scratch=(), aliases=None):
    moved_bytes = sum(a.size * a.dtype.itemsize for a in args)
    return pl.pallas_call(
        kernel,
        out_shape=out,
        in_specs=specs,
        out_specs=jax.tree.map(lambda _: VMEM, out),
        scratch_shapes=list(scratch),
        input_output_aliases=aliases or {},
        cost_estimate=pl.CostEstimate(
            flops=flops, bytes_accessed=moved_bytes, transcendentals=0
        ),
        compiler_params=pltpu.CompilerParams(vmem_limit_bytes=limit * MIB),
    )(*args)


def lanes(shape):
    return lax.broadcasted_iota(jnp.int32, shape, len(shape) - 1)


def rows(shape):
    return lax.broadcasted_iota(jnp.int32, shape, len(shape) - 2)


def dot(a, b):
    return jnp.dot(a, b, preferred_element_type=F32)


def norm_kernel(tokens, gain, sent, normed, held, scale, sems):
    del sent
    first = pltpu.make_async_copy(gain, scale, sems.at[4])
    first.start()
    copies = [
        pltpu.make_async_copy(
            tokens.at[r * 64 : (r + 1) * 64], held.at[r * 64 : (r + 1) * 64], sems.at[r]
        )
        for r in range(4)
    ]
    for copy in copies:
        copy.start()
    first.wait()
    for r in range(4):
        copies[r].wait()
        wide = held[r * 64 : (r + 1) * 64, :].astype(F32)
        meansq = jnp.mean(wide * wide, axis=1, keepdims=True)
        normed[r * 64 : (r + 1) * 64, :] = (
            wide * lax.rsqrt(meansq + 1e-05) * scale[...]
        ).astype(BF)


def adam_kernel(
    place,
    master_hbm,
    moment1_hbm,
    moment2_hbm,
    gradient_hbm,
    pos_hbm,
    nm,
    n1,
    n2,
    s0,
    s1,
    s2,
    s3,
    held,
    pos,
    sems,
):
    copies = [
        pltpu.make_async_copy(ref, held.at[i], sems.at[i])
        for i, ref in enumerate((master_hbm, moment1_hbm, moment2_hbm, gradient_hbm))
    ]
    copies.append(pltpu.make_async_copy(pos_hbm, pos, sems.at[4]))
    for copy in copies:
        copy.start()
    for copy in copies:
        copy.wait()
    g = held[3]
    m1 = beta_one * held[1] + (1.0 - beta_one) * g
    m2 = beta_two * held[2] + (1.0 - beta_two) * g * g
    update = m1 / (1.0 - beta_one**STEP) / (jnp.sqrt(m2 / (1.0 - beta_two**STEP)) + epsilon)
    old = held[0]
    new = old - learn_rate * (update + decay_rate * old)
    nm[...] = new
    n1[...] = m1
    n2[...] = m2
    low = lanes((8, 128)) < 64
    line = rows((8, 128))
    digits = jnp.zeros((8, 128), F32)
    for u in range(2):
        p = pos[:, u * 128 : (u + 1) * 128]
        hi = lax.shift_right_logical(p, 6).astype(F32)
        lo = lax.bitwise_and(p, 63).astype(F32)
        digits = jnp.where(line == u, hi, jnp.where(line == 2 + u, lo, digits))
    rounded = new.astype(BF).astype(F32)
    parts = []
    for h in range(4):
        at = (h // 2) * 128
        kt = rounded[:, 1024 + at : 1152 + at]
        vt = rounded[:, 1280 + at : 1408 + at]
        if h % 2 == 0:
            kv = jnp.where(low, kt, pltpu.roll(vt, 64, 1))
        else:
            kv = jnp.where(low, pltpu.roll(kt, 64, 1), vt)
        parts.append(
            jnp.concatenate(
                [
                    rounded[:, h * 256 : (h + 1) * 256],
                    kv,
                    rounded[:, 1536 + h * 256 : 1792 + h * 256],
                    digits,
                ],
                axis=1,
            )
        )
    ctx = place[1]
    mine = lax.div(ctx, 16) * 2 + lax.rem(ctx, 2)
    for s, ref in enumerate((s0, s1, s2, s3)):
        h = lax.bitwise_xor(mine, s)
        lower = jnp.where(h == 0, parts[0], parts[1])
        upper = jnp.where(h == 2, parts[2], parts[3])
        ref[...] = jnp.where(h < 2, lower, upper)


def repeat_kernel(r0, r1, r2, r3, out):
    block = jnp.concatenate([r0[...], r1[...], r2[...], r3[...]], axis=0).astype(BF)
    for z in range(8):
        out[z * 32 : (z + 1) * 32, :] = block


def place_kernel(place, mixed, qkv, out, posd):
    ctx = place[1]
    y_hi, core = lax.div(ctx, 16), lax.rem(ctx, 2)
    i = rows((256, 256))
    j = lax.shift_right_logical(i, 3)
    slot = lax.bitwise_xor(lax.shift_right_logical(j, 4), y_hi) * 2 + lax.bitwise_xor(
        lax.bitwise_and(j, 1), core
    )
    z = lax.bitwise_and(lax.shift_right_logical(j, 1), 7)
    source = z * 32 + slot * 8 + lax.bitwise_and(i, 7)
    pick = jnp.where(lanes((256, 256)) == source, 1.0, 0.0).astype(BF)
    result = dot(pick, mixed[...])
    qkv[...] = result[:, :384].astype(BF)
    out[...] = result[:, 384:640].astype(BF)
    posd[...] = result[:, 640:]


def order_kernel(place, posd, perm, posq, posk, counts):
    ctx = place[1]

    def pieces(j):
        eight = posd[pl.ds(pl.multiple_of(j * 8, 8), 8), :]
        return [(eight[u : u + 1, :], eight[2 + u : 3 + u, :]) for u in range(2)]

    digits = []
    for other in (0, 1, 16, 17):
        digits += pieces(lax.bitwise_xor(ctx, other))
    row = [hi * 64.0 + lo for hi, lo in digits]
    col = [jnp.broadcast_to(r, (128, 128)).T for r in row]
    at_row = rows((128, 128)).astype(F32)
    for b in range(8):
        below = jnp.zeros((128, 128), F32)
        for a in range(8):
            below = below + jnp.where(col[a] < row[b], 1.0, 0.0)
        rank = jnp.sum(below, axis=0, keepdims=True)
        for a in range(8):
            perm[a * 128 : (a + 1) * 128, b * 128 : (b + 1) * 128] = jnp.where(
                at_row + float(a * 128) == rank, 1.0, 0.0
            ).astype(BF)
    line = rows((16, 1024))
    high = jnp.concatenate([hi for hi, _ in digits], axis=1)
    low = jnp.concatenate([lo for _, lo in digits], axis=1)
    both = jnp.where(line == 0, high, jnp.where(line == 1, low, 0.0)).astype(BF)
    both = lax.dot_general(
        both, perm[...], (((1,), (1,)), ((), ())), preferred_element_type=F32
    )
    ordered = both[0:1] * 64.0 + both[1:2]
    line = rows((8, 128))
    lane = lanes((8, 128))
    most = jnp.zeros((8, 128), F32)
    for c in range(8):
        posk[c : c + 1, :] = ordered[:, c * 128 : (c + 1) * 128]
    for t in range(TILES):
        tile = ordered[:, t * 256 : (t + 1) * 256]
        posq[t * 8 : (t + 1) * 8, :] = jnp.broadcast_to(
            jnp.concatenate([tile] * 4, axis=1), (8, WIDE)
        )
        top = jnp.max(tile[:, 128:], axis=1, keepdims=True)
        most = jnp.where(line == t, jnp.broadcast_to(top, (8, 128)), most)
    result = jnp.zeros((8, 128), F32)
    for z in range(8):
        some = jnp.zeros((8, 128), F32)
        for other in (0, 1, 16, 17):
            for hi, lo in pieces(z * 2 + other):
                some = some + jnp.where(hi * 64.0 + lo <= most, 1.0, 0.0)
        result = jnp.where(lane == z, jnp.sum(some, axis=1, keepdims=True), result)
    counts[...] = result.astype(jnp.int32)


def project(place, tokens, weights, s):
    dp = place[0]
    y_lo, x = lax.div(dp, 4), lax.rem(dp, 4)
    total = None
    for n, block in enumerate(weights):
        other = lax.rem(x + (0, 3, 1, 2)[n % 4], 4)
        owner = (y_lo if n < 4 else 1 - y_lo) * 4 + other
        part = tokens[s][:, pl.ds(pl.multiple_of(owner * 256, 256), 256)]
        term = dot(part, block[...])
        total = term if total is None else total + term
    return total.astype(BF)


def project_kernel(place, perm, posk, t0, t1, t2, t3, *refs):
    weights = refs[:8]
    out, queries, held = refs[8:]
    for s in range(4):
        held[s * 256 : (s + 1) * 256, :] = project(place, (t0, t1, t2, t3), weights, s)
    low = lanes((256, 128)) < 64
    p = posk[...]
    high = jnp.floor(p * (1.0 / 64.0))
    rest = p - high * 64.0
    none = jnp.zeros((4, 128), F32)
    kept = None
    for t in range(TILES):
        u = t // 2
        at = u * HALF
        ordered = dot(perm[t * 256 : (t + 1) * 256, :], held[...])
        kv = ordered[:, 256:]
        if t % 2 == 0:
            kept = kv
        else:
            out[at : at + 256, :] = jnp.where(low, kept, pltpu.roll(kv, 64, 1)).astype(BF)
        for i in range(2):
            c = (t % 2) * 2 + i
            out[at + 256 + c * 64 : at + 320 + c * 64, :] = kv[
                i * 128 : (i + 1) * 128
            ].T[64:].astype(BF)
            for j in range(2):
                q = ordered[i * 128 : (i + 1) * 128, j * 128 : (j + 1) * 128].T * 0.125
                for e in range(2):
                    lane = (j * 2 + e) * 256 + i * 128
                    queries[t * 64 : (t + 1) * 64, lane : lane + 128] = q[
                        e * 64 : (e + 1) * 64
                    ].astype(BF)
    for u in range(2):
        digits = jnp.concatenate(
            [high[u * 4 : u * 4 + 4], none, rest[u * 4 : u * 4 + 4], none], axis=0
        )
        out[u * HALF + 512 : (u + 1) * HALF, :] = digits.astype(BF)


def attend_kernel(blocks, first, last, *refs):
    refs = list(refs)
    place, counts, q, posq = refs[:4]
    del refs[:4]
    n_refs = 1 + max(n for _, halves in blocks for n, _ in halves)
    held = refs[:n_refs]
    del refs[:n_refs]
    if not first:
        m_in, acc_in = refs[:2]
        del refs[:2]
    if last:
        perm = refs.pop(0)
        outs = refs[:4]
        del refs[:4]
        kk, v1, pk, scores, mixed = refs
    else:
        m_ref, acc_ref, kk, v1, pk, scores = refs
    lines = []
    n = 0
    for _, halves in blocks:
        for ref, at in halves:
            a = held[ref][at : at + 256, :].astype(F32)
            b = pltpu.roll(a, 64, 1)
            kk[n * 512 : n * 512 + 256, :] = a.astype(BF)
            kk[n * 512 + 256 : n * 512 + 512, :] = b.astype(BF)
            for c in range(4):
                v1[0:64, n * 512 + c * 128 : n * 512 + (c + 1) * 128] = held[ref][
                    at + 256 + c * 64 : at + 320 + c * 64, :
                ]
            digits = held[ref][at + 512 : at + HALF, :].astype(F32)
            lines.append(digits[0:8] * 64.0 + digits[8:16])
            n += 1
    v1[64:80, :] = jnp.ones((16, n * 512), BF)
    lines.append(jnp.zeros((128 - 8 * n, 128), F32))
    columns = jnp.concatenate(lines, axis=0).T
    for i in range(n):
        for c in range(4):
            k = i * 4 + c
            pk[k * 128 : (k + 1) * 128, :] = jnp.broadcast_to(
                columns[:, i * 8 + c : i * 8 + c + 1], (128, 128)
            )
    z = lax.rem(lax.div(place[1], 2), 8)

    def tile_step(t, _):
        qt = q[pl.ds(pl.multiple_of(t * 64, 64), 64), :]
        pq = posq[pl.ds(pl.multiple_of(t * 8, 8), 8), :][0:1]
        m_at = pl.ds(pl.multiple_of(t * 8, 8), 8)
        acc_at = pl.ds(pl.multiple_of(t * 80, 16), 80)
        if first:
            m = jnp.full((1, WIDE), -1e29, F32)
            acc = jnp.zeros((80, WIDE), F32)
        else:
            m = m_in[m_at, :][0:1]
            acc = acc_in[acc_at, :]

        def some(base, steps, state):
            m, acc = state
            high = m
            chunks = [(j * KEYS, KEYS) for j in range(steps)]
            for off, size in chunks:
                at = base + off
                s = dot(kk[at : at + size, 0:64], qt)
                line = jnp.concatenate([pk[at : at + size, :]] * (WIDE // 128), axis=1)
                s = jnp.where(line <= pq, s, -1e30)
                scores[off : off + size, :] = s
                high = jnp.maximum(high, jnp.max(s, axis=0, keepdims=True))
            acc = acc * jnp.exp(m - high)
            for off, size in chunks:
                at = base + off
                p = jnp.exp(scores[off : off + size, :] - high).astype(BF)
                acc = acc + dot(v1[:, at : at + size], p)
            return high, acc

        state = (m, acc)
        for i, (away, _) in enumerate(blocks):
            other = lax.rem(z + away + 8, 8)
            steps = lax.div(counts[t, other] + (KEYS - 1), KEYS)
            branches = [functools.partial(some, i * 1024, k) for k in range(1024 // KEYS + 1)]
            branches[0] = lambda state: state
            state = lax.switch(steps, branches, state)
        m, acc = state
        if last:
            o = acc[0:64] / acc[64:65]
            for h in range(4):
                mixed[h * 64 : (h + 1) * 64, pl.ds(pl.multiple_of(t * 256, 256), 256)] = o[
                    :, h * 256 : (h + 1) * 256
                ].astype(BF)
        else:
            m_ref[m_at, :] = jnp.broadcast_to(m, (8, WIDE))
            acc_ref[acc_at, :] = acc
        return 0

    lax.fori_loop(0, TILES, tile_step, 0)
    if last:
        for s in range(4):
            back = dot(mixed[...], perm[:, s * 256 : (s + 1) * 256])
            outs[s][...] = back.T.astype(BF)


def out_kernel(half, last, *refs):
    place, a0, a1, w_own, w_core = refs[:5]
    dp = place[0]
    y_lo, x = lax.div(dp, 4), lax.rem(dp, 4)
    out = refs[-1]
    for n, step in enumerate((0, 3, 1, 2)):
        other = lax.rem(x + step, 4)
        for r in range(2):
            owner = (y_lo if r == 0 else 1 - y_lo) * 4 + other
            to = pl.ds(pl.multiple_of(owner * 256, 256), 256)
            at = n * 1024 + r * 512 + half * 256
            total = refs[5][:, to] if last else None
            for a, w in ((a0, w_own), (a1, w_core)):
                term = lax.dot_general(
                    a[...], w[at : at + 256, :], (((1,), (1,)), ((), ())), preferred_element_type=F32
                )
                total = term if total is None else total + term
            out[:, to] = total.astype(out.dtype)


def after(value, other):
    return lax.optimization_barrier((value, other))[0]


def spread(pair):
    return pair, send(pair, X_UP), send(pair, X_DOWN), send(pair, X_FAR)


def attend(place, counts, q, posq, held, blocks, state, perm=None):
    first, last = state is None, perm is not None
    args = [place, counts, q, posq, *held]
    specs = [SMEM, SMEM] + [VMEM] * (2 + len(held))
    aliases = {}
    if not first:
        if not last:
            aliases = {len(args): 0, len(args) + 1: 1}
        args += state
        specs += [VMEM] * 2
    n = len(blocks)
    scratch = [
        pltpu.VMEM((n * 1024, 128), BF),
        pltpu.VMEM((80, n * 1024), BF),
        pltpu.VMEM((n * 1024, 128), F32),
        pltpu.VMEM((1024, WIDE), F32),
    ]
    if last:
        args.append(perm)
        specs.append(VMEM)
        out = [jax.ShapeDtypeStruct((256, 256), BF)] * 4
        scratch.append(pltpu.VMEM((256, 1024), BF))
    else:
        out = [
            jax.ShapeDtypeStruct((TILES * 8, WIDE), F32),
            jax.ShapeDtypeStruct((TILES * 80, WIDE), F32),
        ]
    return call(
        functools.partial(attend_kernel, blocks, first, last),
        out,
        args,
        specs,
        flops=n * 4096 * 1024 * 64 * 8,
        scratch=scratch,
        aliases=aliases,
    )


def body(master, moment1, moment2, gradient, tokens, gain, positions):
    place = jnp.stack([lax.axis_index("dp"), lax.axis_index("ctx")]).astype(jnp.int32)
    shard = jax.ShapeDtypeStruct(master.shape, F32)
    slot = jax.ShapeDtypeStruct((8, 768), F32)
    new_master, new_moment1, new_moment2, *sent = call(
        adam_kernel,
        [shard, shard, shard, slot, slot, slot, slot],
        [place, master, moment1, moment2, gradient, positions],
        [SMEM] + [HBM] * 5,
        limit=60,
        scratch=[
            pltpu.VMEM((4, 8, 2560), F32),
            pltpu.VMEM((1, 256), jnp.int32),
            pltpu.SemaphoreType.DMA((5,)),
        ],
    )
    group = [sent[0], send(sent[1], CORE), send(sent[2], Y_HI), send(sent[3], DIAG)]
    normed = call(
        norm_kernel,
        jax.ShapeDtypeStruct((256, 2048), BF),
        [tokens.reshape(256, 2048), gain.reshape(1, 2048), sent[0]],
        [HBM] * 2 + [pl.BlockSpec(memory_space=pl.ANY)],
        limit=60,
        scratch=[
            pltpu.VMEM((256, 2048), BF),
            pltpu.VMEM((1, 2048), F32),
            pltpu.SemaphoreType.DMA((5,)),
        ],
    )
    by_y = send(after(normed, group), Y_HI)
    by_core = send(normed, CORE)
    mixed = call(
        repeat_kernel,
        jax.ShapeDtypeStruct((256, 768), BF),
        group,
        [VMEM] * 4,
    )
    along_z = [[y * 16 + z * 2 + c for z in range(8)] for y in range(2) for c in range(2)]
    mixed = lax.all_to_all(mixed, "ctx", 0, 0, tiled=True, axis_index_groups=along_z)
    mine_qkv, mine_out, posd = call(
        place_kernel,
        [
            jax.ShapeDtypeStruct((256, 384), BF),
            jax.ShapeDtypeStruct((256, 256), BF),
            jax.ShapeDtypeStruct((256, 128), F32),
        ],
        [place, mixed],
        [SMEM, VMEM],
    )
    perm, posq, posk, counts = call(
        order_kernel,
        [
            jax.ShapeDtypeStruct((1024, 1024), BF),
            jax.ShapeDtypeStruct((TILES * 8, WIDE), F32),
            jax.ShapeDtypeStruct((8, 128), F32),
            jax.ShapeDtypeStruct((8, 128), jnp.int32),
        ],
        [place, posd],
        [SMEM, VMEM],
    )
    near = send(mine_qkv, Y_LO)
    own = spread(mine_qkv)
    slots = [normed, by_core, by_y, send(after(by_y, (own, near, counts)), CORE)]
    weights = own + spread(after(near, (counts, by_core)))
    block, q = call(
        project_kernel,
        [
            jax.ShapeDtypeStruct((2 * HALF, 128), BF),
            jax.ShapeDtypeStruct((TILES * 64, WIDE), BF),
        ],
        [place, perm, posk, *slots, *weights],
        [SMEM] + [VMEM] * 14,
        flops=2 * 1024 * 3072 * 384,
        scratch=[pltpu.VMEM((1024, 384), BF)],
    )
    near_out = send(after(mine_out, weights[1]), Y_HI)
    out_pair = jnp.concatenate([mine_out, after(near_out, weights[5:])], axis=0)
    out_pair = jnp.concatenate([out_pair, send(out_pair, Y_LO)], axis=0)

    def whole(ref):
        return ((ref, 0), (ref, HALF))

    state = attend(place, counts, q, posq, [block], [(0, whole(0))], None)
    up, down = block, block
    for step in range(1, 4):
        up, down = send(up, Z_UP), send(down, Z_DOWN)
        if step == 1:
            out_own = jnp.concatenate(spread(after(out_pair, (up, down, state[0]))), axis=0)
        state = attend(
            place, counts, q, posq, [up, down], [(-step, whole(0)), (step, whole(1))], state
        )
    far = send(up, Z_UP)
    out_core = send(after(out_own, (far, state[0])), CORE)
    parts = attend(place, counts, q, posq, [far], [(4, whole(0))], state, perm)
    by_y, by_both, by_core = send(parts[2], Y_HI), send(parts[3], DIAG), send(parts[1], CORE)
    flops = 256 * 1024 * 2048
    half = call(
        functools.partial(out_kernel, 0, False),
        jax.ShapeDtypeStruct((256, 2048), F32),
        [place, parts[0], by_core, out_own, out_core],
        [SMEM] + [VMEM] * 4,
        flops=flops,
    )
    block_out = call(
        functools.partial(out_kernel, 1, True),
        jax.ShapeDtypeStruct((256, 2048), BF),
        [place, by_y, by_both, out_own, out_core, half],
        [SMEM] + [VMEM] * 5,
        flops=flops,
    )
    return new_master, new_moment1, new_moment2, block_out.reshape(1, 256, 2048)


def solution(mesh):
    rows_split = P(AXES, None)
    return jax.shard_map(
        body,
        mesh=mesh,
        in_specs=(
            rows_split,
            rows_split,
            rows_split,
            rows_split,
            P("dp", "ctx", None),
            P(),
            P("dp", "ctx"),
        ),
        out_specs=(rows_split, rows_split, rows_split, P("dp", "ctx", None)),
        check_vma=False,
    )
```

```python
import functools

import jax
import jax.numpy as jnp
from jax import lax
from jax.experimental import pallas as pl
from jax.experimental.pallas import tpu as pltpu
from jax.sharding import PartitionSpec as P

STEP = 100
beta_one = 0.9
beta_two = 0.95
learn_rate = 0.002
decay_rate = 0.1
epsilon = 1e-08

AXES = ("dp", "ctx")
BF = jnp.bfloat16
F32 = jnp.float32
MIB = 1 << 20
HALF = 528
TILES = 4
WIDE = 1024
KEYS = 256


def device_of(x, y, z, core):
    x, y, z = x % 4, y % 4, z % 8
    return ((y % 2) * 4 + x) * 32 + (y // 2) * 16 + z * 2 + core


def moved(target):
    return [
        (device_of(x, y, z, c), device_of(*target(x, y, z, c)))
        for x in range(4)
        for y in range(4)
        for z in range(8)
        for c in range(2)
    ]


CORE = moved(lambda x, y, z, c: (x, y, z, 1 - c))
Y_HI = moved(lambda x, y, z, c: (x, y + 2, z, c))
DIAG = moved(lambda x, y, z, c: (x, y + 2, z, 1 - c))
Y_LO = moved(lambda x, y, z, c: (x, y ^ 1, z, c))
X_UP = moved(lambda x, y, z, c: (x + 1, y, z, c))
X_DOWN = moved(lambda x, y, z, c: (x - 1, y, z, c))
X_FAR = moved(lambda x, y, z, c: (x + 2, y, z, c))
Z_UP = moved(lambda x, y, z, c: (x, y, z + 1, c))
Z_DOWN = moved(lambda x, y, z, c: (x, y, z - 1, c))


def send(value, perm):
    return lax.ppermute(value, AXES, perm)


VMEM = pl.BlockSpec(memory_space=pltpu.VMEM)
SMEM = pl.BlockSpec(memory_space=pltpu.SMEM)
HBM = pl.BlockSpec(memory_space=pltpu.HBM)


def call(kernel, out, args, specs, limit=32, flops=0, scratch=(), aliases=None):
    moved_bytes = sum(a.size * a.dtype.itemsize for a in args)
    return pl.pallas_call(
        kernel,
        out_shape=out,
        in_specs=specs,
        out_specs=jax.tree.map(lambda _: VMEM, out),
        scratch_shapes=list(scratch),
        input_output_aliases=aliases or {},
        cost_estimate=pl.CostEstimate(
            flops=flops, bytes_accessed=moved_bytes, transcendentals=0
        ),
        compiler_params=pltpu.CompilerParams(vmem_limit_bytes=limit * MIB),
    )(*args)


def lanes(shape):
    return lax.broadcasted_iota(jnp.int32, shape, len(shape) - 1)


def rows(shape):
    return lax.broadcasted_iota(jnp.int32, shape, len(shape) - 2)


def dot(a, b):
    return jnp.dot(a, b, preferred_element_type=F32)


def norm_kernel(tokens, gain, sent, normed, held, scale, sems):
    del sent
    first = pltpu.make_async_copy(gain, scale, sems.at[4])
    first.start()
    copies = [
        pltpu.make_async_copy(
            tokens.at[r * 64 : (r + 1) * 64], held.at[r * 64 : (r + 1) * 64], sems.at[r]
        )
        for r in range(4)
    ]
    for copy in copies:
        copy.start()
    first.wait()
    for r in range(4):
        copies[r].wait()
        wide = held[r * 64 : (r + 1) * 64, :].astype(F32)
        meansq = jnp.mean(wide * wide, axis=1, keepdims=True)
        normed[r * 64 : (r + 1) * 64, :] = (
            wide * lax.rsqrt(meansq + 1e-05) * scale[...]
        ).astype(BF)


def adam_kernel(
    place,
    master_hbm,
    moment1_hbm,
    moment2_hbm,
    gradient_hbm,
    pos_hbm,
    nm,
    n1,
    n2,
    s0,
    s1,
    s2,
    s3,
    held,
    pos,
    sems,
):
    copies = [
        pltpu.make_async_copy(ref, held.at[i], sems.at[i])
        for i, ref in enumerate((master_hbm, moment1_hbm, moment2_hbm, gradient_hbm))
    ]
    copies.append(pltpu.make_async_copy(pos_hbm, pos, sems.at[4]))
    for copy in copies:
        copy.start()
    for copy in copies:
        copy.wait()
    g = held[3]
    m1 = beta_one * held[1] + (1.0 - beta_one) * g
    m2 = beta_two * held[2] + (1.0 - beta_two) * g * g
    update = m1 / (1.0 - beta_one**STEP) / (jnp.sqrt(m2 / (1.0 - beta_two**STEP)) + epsilon)
    old = held[0]
    new = old - learn_rate * (update + decay_rate * old)
    nm[...] = new
    n1[...] = m1
    n2[...] = m2
    low = lanes((8, 128)) < 64
    line = rows((8, 128))
    digits = jnp.zeros((8, 128), F32)
    for u in range(2):
        p = pos[:, u * 128 : (u + 1) * 128]
        hi = lax.shift_right_logical(p, 6).astype(F32)
        lo = lax.bitwise_and(p, 63).astype(F32)
        digits = jnp.where(line == u, hi, jnp.where(line == 2 + u, lo, digits))
    rounded = new.astype(BF).astype(F32)
    parts = []
    for h in range(4):
        at = (h // 2) * 128
        kt = rounded[:, 1024 + at : 1152 + at]
        vt = rounded[:, 1280 + at : 1408 + at]
        if h % 2 == 0:
            kv = jnp.where(low, kt, pltpu.roll(vt, 64, 1))
        else:
            kv = jnp.where(low, pltpu.roll(kt, 64, 1), vt)
        parts.append(
            jnp.concatenate(
                [
                    rounded[:, h * 256 : (h + 1) * 256],
                    kv,
                    rounded[:, 1536 + h * 256 : 1792 + h * 256],
                    digits,
                ],
                axis=1,
            )
        )
    ctx = place[1]
    mine = lax.div(ctx, 16) * 2 + lax.rem(ctx, 2)
    for s, ref in enumerate((s0, s1, s2, s3)):
        h = lax.bitwise_xor(mine, s)
        lower = jnp.where(h == 0, parts[0], parts[1])
        upper = jnp.where(h == 2, parts[2], parts[3])
        ref[...] = jnp.where(h < 2, lower, upper)


def repeat_kernel(r0, r1, r2, r3, out):
    block = jnp.concatenate([r0[...], r1[...], r2[...], r3[...]], axis=0).astype(BF)
    for z in range(8):
        out[z * 32 : (z + 1) * 32, :] = block


def place_kernel(place, mixed, qkv, out, posd):
    ctx = place[1]
    y_hi, core = lax.div(ctx, 16), lax.rem(ctx, 2)
    i = rows((256, 256))
    j = lax.shift_right_logical(i, 3)
    slot = lax.bitwise_xor(lax.shift_right_logical(j, 4), y_hi) * 2 + lax.bitwise_xor(
        lax.bitwise_and(j, 1), core
    )
    z = lax.bitwise_and(lax.shift_right_logical(j, 1), 7)
    source = z * 32 + slot * 8 + lax.bitwise_and(i, 7)
    pick = jnp.where(lanes((256, 256)) == source, 1.0, 0.0).astype(BF)
    result = dot(pick, mixed[...])
    qkv[...] = result[:, :384].astype(BF)
    out[...] = result[:, 384:640].astype(BF)
    posd[...] = result[:, 640:]


def order_kernel(place, posd, perm, posq, posk, counts):
    ctx = place[1]

    def pieces(j):
        eight = posd[pl.ds(pl.multiple_of(j * 8, 8), 8), :]
        return [(eight[u : u + 1, :], eight[2 + u : 3 + u, :]) for u in range(2)]

    digits = []
    for other in (0, 1, 16, 17):
        digits += pieces(lax.bitwise_xor(ctx, other))
    row = [hi * 64.0 + lo for hi, lo in digits]
    col = [jnp.broadcast_to(r, (128, 128)).T for r in row]
    at_row = rows((128, 128)).astype(F32)
    for b in range(8):
        below = jnp.zeros((128, 128), F32)
        for a in range(8):
            below = below + jnp.where(col[a] < row[b], 1.0, 0.0)
        rank = jnp.sum(below, axis=0, keepdims=True)
        for a in range(8):
            perm[a * 128 : (a + 1) * 128, b * 128 : (b + 1) * 128] = jnp.where(
                at_row + float(a * 128) == rank, 1.0, 0.0
            ).astype(BF)
    line = rows((16, 1024))
    high = jnp.concatenate([hi for hi, _ in digits], axis=1)
    low = jnp.concatenate([lo for _, lo in digits], axis=1)
    both = jnp.where(line == 0, high, jnp.where(line == 1, low, 0.0)).astype(BF)
    both = lax.dot_general(
        both, perm[...], (((1,), (1,)), ((), ())), preferred_element_type=F32
    )
    ordered = both[0:1] * 64.0 + both[1:2]
    line = rows((8, 128))
    lane = lanes((8, 128))
    most = jnp.zeros((8, 128), F32)
    for c in range(8):
        posk[c : c + 1, :] = ordered[:, c * 128 : (c + 1) * 128]
    for t in range(TILES):
        tile = ordered[:, t * 256 : (t + 1) * 256]
        posq[t * 8 : (t + 1) * 8, :] = jnp.broadcast_to(
            jnp.concatenate([tile] * 4, axis=1), (8, WIDE)
        )
        top = jnp.max(tile[:, 128:], axis=1, keepdims=True)
        most = jnp.where(line == t, jnp.broadcast_to(top, (8, 128)), most)
    result = jnp.zeros((8, 128), F32)
    for z in range(8):
        some = jnp.zeros((8, 128), F32)
        for other in (0, 1, 16, 17):
            for hi, lo in pieces(z * 2 + other):
                some = some + jnp.where(hi * 64.0 + lo <= most, 1.0, 0.0)
        result = jnp.where(lane == z, jnp.sum(some, axis=1, keepdims=True), result)
    counts[...] = result.astype(jnp.int32)


def project(place, tokens, weights, s):
    dp = place[0]
    y_lo, x = lax.div(dp, 4), lax.rem(dp, 4)
    total = None
    for n, block in enumerate(weights):
        other = lax.rem(x + (0, 3, 1, 2)[n % 4], 4)
        owner = (y_lo if n < 4 else 1 - y_lo) * 4 + other
        part = tokens[s][:, pl.ds(pl.multiple_of(owner * 256, 256), 256)]
        term = dot(part, block[...])
        total = term if total is None else total + term
    return total.astype(BF)


def project_kernel(place, perm, posk, t0, t1, t2, t3, *refs):
    weights = refs[:8]
    out, queries, held = refs[8:]
    for s in range(4):
        held[s * 256 : (s + 1) * 256, :] = project(place, (t0, t1, t2, t3), weights, s)
    low = lanes((256, 128)) < 64
    p = posk[...]
    high = jnp.floor(p * (1.0 / 64.0))
    rest = p - high * 64.0
    none = jnp.zeros((4, 128), F32)
    kept = None
    for t in range(TILES):
        u = t // 2
        at = u * HALF
        ordered = dot(perm[t * 256 : (t + 1) * 256, :], held[...])
        kv = ordered[:, 256:]
        if t % 2 == 0:
            kept = kv
        else:
            out[at : at + 256, :] = jnp.where(low, kept, pltpu.roll(kv, 64, 1)).astype(BF)
        for i in range(2):
            c = (t % 2) * 2 + i
            out[at + 256 + c * 64 : at + 320 + c * 64, :] = kv[
                i * 128 : (i + 1) * 128
            ].T[64:].astype(BF)
            for j in range(2):
                q = ordered[i * 128 : (i + 1) * 128, j * 128 : (j + 1) * 128].T * 0.125
                for e in range(2):
                    lane = (j * 2 + e) * 256 + i * 128
                    queries[t * 64 : (t + 1) * 64, lane : lane + 128] = q[
                        e * 64 : (e + 1) * 64
                    ].astype(BF)
    for u in range(2):
        digits = jnp.concatenate(
            [high[u * 4 : u * 4 + 4], none, rest[u * 4 : u * 4 + 4], none], axis=0
        )
        out[u * HALF + 512 : (u + 1) * HALF, :] = digits.astype(BF)


def attend_kernel(blocks, first, last, *refs):
    refs = list(refs)
    place, counts, q, posq = refs[:4]
    del refs[:4]
    n_refs = 1 + max(n for _, halves in blocks for n, _ in halves)
    held = refs[:n_refs]
    del refs[:n_refs]
    if not first:
        m_in, acc_in = refs[:2]
        del refs[:2]
    if last:
        perm = refs.pop(0)
        outs = refs[:4]
        del refs[:4]
        kk, v1, pk, scores, mixed = refs
    else:
        m_ref, acc_ref, kk, v1, pk, scores = refs
    lines = []
    n = 0
    for _, halves in blocks:
        for ref, at in halves:
            a = held[ref][at : at + 256, :].astype(F32)
            b = pltpu.roll(a, 64, 1)
            kk[n * 512 : n * 512 + 256, :] = a.astype(BF)
            kk[n * 512 + 256 : n * 512 + 512, :] = b.astype(BF)
            for c in range(4):
                v1[0:64, n * 512 + c * 128 : n * 512 + (c + 1) * 128] = held[ref][
                    at + 256 + c * 64 : at + 320 + c * 64, :
                ]
            digits = held[ref][at + 512 : at + HALF, :].astype(F32)
            lines.append(digits[0:8] * 64.0 + digits[8:16])
            n += 1
    v1[64:80, :] = jnp.ones((16, n * 512), BF)
    lines.append(jnp.zeros((128 - 8 * n, 128), F32))
    columns = jnp.concatenate(lines, axis=0).T
    for i in range(n):
        for c in range(4):
            k = i * 4 + c
            pk[k * 128 : (k + 1) * 128, :] = jnp.broadcast_to(
                columns[:, i * 8 + c : i * 8 + c + 1], (128, 128)
            )
    z = lax.rem(lax.div(place[1], 2), 8)

    def tile_step(t, _):
        qt = q[pl.ds(pl.multiple_of(t * 64, 64), 64), :]
        pq = posq[pl.ds(pl.multiple_of(t * 8, 8), 8), :][0:1]
        m_at = pl.ds(pl.multiple_of(t * 8, 8), 8)
        acc_at = pl.ds(pl.multiple_of(t * 80, 16), 80)
        if first:
            m = jnp.full((1, WIDE), -1e29, F32)
            acc = jnp.zeros((80, WIDE), F32)
        else:
            m = m_in[m_at, :][0:1]
            acc = acc_in[acc_at, :]

        def some(base, steps, state):
            m, acc = state
            high = m
            chunks = [(j * KEYS, KEYS) for j in range(steps)]
            for off, size in chunks:
                at = base + off
                s = dot(kk[at : at + size, 0:64], qt)
                line = jnp.concatenate([pk[at : at + size, :]] * (WIDE // 128), axis=1)
                s = jnp.where(line <= pq, s, -1e30)
                scores[off : off + size, :] = s
                high = jnp.maximum(high, jnp.max(s, axis=0, keepdims=True))
            acc = acc * jnp.exp(m - high)
            for off, size in chunks:
                at = base + off
                p = jnp.exp(scores[off : off + size, :] - high).astype(BF)
                acc = acc + dot(v1[:, at : at + size], p)
            return high, acc

        state = (m, acc)
        for i, (away, _) in enumerate(blocks):
            other = lax.rem(z + away + 8, 8)
            steps = lax.div(counts[t, other] + (KEYS - 1), KEYS)
            branches = [functools.partial(some, i * 1024, k) for k in range(1024 // KEYS + 1)]
            branches[0] = lambda state: state
            state = lax.switch(steps, branches, state)
        m, acc = state
        if last:
            o = acc[0:64] / acc[64:65]
            for h in range(4):
                mixed[h * 64 : (h + 1) * 64, pl.ds(pl.multiple_of(t * 256, 256), 256)] = o[
                    :, h * 256 : (h + 1) * 256
                ].astype(BF)
        else:
            m_ref[m_at, :] = jnp.broadcast_to(m, (8, WIDE))
            acc_ref[acc_at, :] = acc
        return 0

    lax.fori_loop(0, TILES, tile_step, 0)
    if last:
        for s in range(4):
            back = dot(mixed[...], perm[:, s * 256 : (s + 1) * 256])
            outs[s][...] = back.T.astype(BF)


def out_kernel(half, last, *refs):
    place, a0, a1, w_own, w_core = refs[:5]
    dp = place[0]
    y_lo, x = lax.div(dp, 4), lax.rem(dp, 4)
    out = refs[-1]
    for n, step in enumerate((0, 3, 1, 2)):
        other = lax.rem(x + step, 4)
        for r in range(2):
            owner = (y_lo if r == 0 else 1 - y_lo) * 4 + other
            to = pl.ds(pl.multiple_of(owner * 256, 256), 256)
            at = n * 1024 + r * 512 + half * 256
            total = refs[5][:, to] if last else None
            for a, w in ((a0, w_own), (a1, w_core)):
                term = lax.dot_general(
                    a[...], w[at : at + 256, :], (((1,), (1,)), ((), ())), preferred_element_type=F32
                )
                total = term if total is None else total + term
            out[:, to] = total.astype(out.dtype)


def after(value, other):
    return lax.optimization_barrier((value, other))[0]


def spread(pair):
    return pair, send(pair, X_UP), send(pair, X_DOWN), send(pair, X_FAR)


def attend(place, counts, q, posq, held, blocks, state, perm=None):
    first, last = state is None, perm is not None
    args = [place, counts, q, posq, *held]
    specs = [SMEM, SMEM] + [VMEM] * (2 + len(held))
    aliases = {}
    if not first:
        if not last:
            aliases = {len(args): 0, len(args) + 1: 1}
        args += state
        specs += [VMEM] * 2
    n = len(blocks)
    scratch = [
        pltpu.VMEM((n * 1024, 128), BF),
        pltpu.VMEM((80, n * 1024), BF),
        pltpu.VMEM((n * 1024, 128), F32),
        pltpu.VMEM((1024, WIDE), F32),
    ]
    if last:
        args.append(perm)
        specs.append(VMEM)
        out = [jax.ShapeDtypeStruct((256, 256), BF)] * 4
        scratch.append(pltpu.VMEM((256, 1024), BF))
    else:
        out = [
            jax.ShapeDtypeStruct((TILES * 8, WIDE), F32),
            jax.ShapeDtypeStruct((TILES * 80, WIDE), F32),
        ]
    return call(
        functools.partial(attend_kernel, blocks, first, last),
        out,
        args,
        specs,
        flops=n * 4096 * 1024 * 64 * 8,
        scratch=scratch,
        aliases=aliases,
    )


def body(master, moment1, moment2, gradient, tokens, gain, positions):
    place = jnp.stack([lax.axis_index("dp"), lax.axis_index("ctx")]).astype(jnp.int32)
    shard = jax.ShapeDtypeStruct(master.shape, F32)
    slot = jax.ShapeDtypeStruct((8, 768), F32)
    new_master, new_moment1, new_moment2, *sent = call(
        adam_kernel,
        [shard, shard, shard, slot, slot, slot, slot],
        [place, master, moment1, moment2, gradient, positions],
        [SMEM] + [HBM] * 5,
        limit=60,
        scratch=[
            pltpu.VMEM((4, 8, 2560), F32),
            pltpu.VMEM((1, 256), jnp.int32),
            pltpu.SemaphoreType.DMA((5,)),
        ],
    )
    group = [sent[0], send(sent[1], CORE), send(sent[2], Y_HI), send(sent[3], DIAG)]
    normed = call(
        norm_kernel,
        jax.ShapeDtypeStruct((256, 2048), BF),
        [tokens.reshape(256, 2048), gain.reshape(1, 2048), sent[0]],
        [HBM] * 2 + [pl.BlockSpec(memory_space=pl.ANY)],
        limit=60,
        scratch=[
            pltpu.VMEM((256, 2048), BF),
            pltpu.VMEM((1, 2048), F32),
            pltpu.SemaphoreType.DMA((5,)),
        ],
    )
    by_y = send(after(normed, group), Y_HI)
    by_core = send(normed, CORE)
    mixed = call(
        repeat_kernel,
        jax.ShapeDtypeStruct((256, 768), BF),
        group,
        [VMEM] * 4,
    )
    along_z = [[y * 16 + z * 2 + c for z in range(8)] for y in range(2) for c in range(2)]
    mixed = lax.all_to_all(mixed, "ctx", 0, 0, tiled=True, axis_index_groups=along_z)
    mine_qkv, mine_out, posd = call(
        place_kernel,
        [
            jax.ShapeDtypeStruct((256, 384), BF),
            jax.ShapeDtypeStruct((256, 256), BF),
            jax.ShapeDtypeStruct((256, 128), F32),
        ],
        [place, mixed],
        [SMEM, VMEM],
    )
    perm, posq, posk, counts = call(
        order_kernel,
        [
            jax.ShapeDtypeStruct((1024, 1024), BF),
            jax.ShapeDtypeStruct((TILES * 8, WIDE), F32),
            jax.ShapeDtypeStruct((8, 128), F32),
            jax.ShapeDtypeStruct((8, 128), jnp.int32),
        ],
        [place, posd],
        [SMEM, VMEM],
    )
    near = send(mine_qkv, Y_LO)
    own = spread(mine_qkv)
    slots = [normed, by_core, by_y, send(after(by_y, (own, near, counts)), CORE)]
    weights = own + spread(after(near, counts))
    block, q = call(
        project_kernel,
        [
            jax.ShapeDtypeStruct((2 * HALF, 128), BF),
            jax.ShapeDtypeStruct((TILES * 64, WIDE), BF),
        ],
        [place, perm, posk, *slots, *weights],
        [SMEM] + [VMEM] * 14,
        flops=2 * 1024 * 3072 * 384,
        scratch=[pltpu.VMEM((1024, 384), BF)],
    )
    mine_out = after(mine_out, weights[1])
    out_pair = jnp.concatenate([mine_out, send(mine_out, Y_HI)], axis=0)
    out_pair = jnp.concatenate([out_pair, send(out_pair, Y_LO)], axis=0)

    def whole(ref):
        return ((ref, 0), (ref, HALF))

    state = attend(place, counts, q, posq, [block], [(0, whole(0))], None)
    up, down = block, block
    for step in range(1, 4):
        up, down = send(up, Z_UP), send(down, Z_DOWN)
        if step == 1:
            out_own = jnp.concatenate(spread(after(out_pair, (up, down, state[0]))), axis=0)
        state = attend(
            place, counts, q, posq, [up, down], [(-step, whole(0)), (step, whole(1))], state
        )
    far = send(up, Z_UP)
    out_core = send(after(out_own, (far, state[0])), CORE)
    parts = attend(place, counts, q, posq, [far], [(4, whole(0))], state, perm)
    by_y, by_both, by_core = send(parts[2], Y_HI), send(parts[3], DIAG), send(parts[1], CORE)
    flops = 256 * 1024 * 2048
    half = call(
        functools.partial(out_kernel, 0, False),
        jax.ShapeDtypeStruct((256, 2048), F32),
        [place, parts[0], by_core, out_own, out_core],
        [SMEM] + [VMEM] * 4,
        flops=flops,
    )
    block_out = call(
        functools.partial(out_kernel, 1, True),
        jax.ShapeDtypeStruct((256, 2048), BF),
        [place, by_y, by_both, out_own, out_core, half],
        [SMEM] + [VMEM] * 5,
        flops=flops,
    )
    return new_master, new_moment1, new_moment2, block_out.reshape(1, 256, 2048)


def solution(mesh):
    rows_split = P(AXES, None)
    return jax.shard_map(
        body,
        mesh=mesh,
        in_specs=(
            rows_split,
            rows_split,
            rows_split,
            rows_split,
            P("dp", "ctx", None),
            P(),
            P("dp", "ctx"),
        ),
        out_specs=(rows_split, rows_split, rows_split, P("dp", "ctx", None)),
        check_vma=False,
    )
```
